32 devices in a mesh: section: 2 (over core), dp: 8 (over z, x), tensor: 2 (over y).
Axes of the slice: x: 2, y: 2, z: 4, core: 2. Of those that a mesh axis runs over, the one named last changes fastest.
Arguments:
- ends_in: bfloat16 [2, 16, 1024, 768], P('section', 'dp', 'tensor'), may hold values from -6 to 6
- lengths: int32 [16], P('dp'), may hold values from 256 to 1024, as said below
- vectors: float32 [2, 12, 768], P('section', None, ('dp', 'tensor')), may hold values from -1.5 to 1.5
- w_qkv: bfloat16 [2, 768, 3, 768], P('section', 'dp', None, 'tensor'), may hold values from -0.21875 to 0.21875
- w_out: bfloat16 [2, 768, 768], P('section', 'tensor', 'dp'), may hold values from -0.875 to 0.875
- w_up: bfloat16 [2, 768, 3072], P('section', 'dp', 'tensor'), may hold values from -0.21875 to 0.21875
- w_down: bfloat16 [2, 3072, 768], P('section', 'tensor', 'dp'), may hold values from -0.109375 to 0.109375
Outputs:
- boundary: float32 [2, 16, 1024, 768], P('section', 'dp', 'tensor')
- vectors_grad: float32 [2, 12, 768], P('section', None, ('dp', 'tensor'))
- w_qkv_grad: float32 [2, 768, 3, 768], P('section', 'dp', None, 'tensor')
- w_out_grad: float32 [2, 768, 768], P('section', 'tensor', 'dp')
- w_up_grad: float32 [2, 768, 3072], P('section', 'dp', 'tensor')
- w_down_grad: float32 [2, 3072, 768], P('section', 'tensor', 'dp')
The draws below stay inside these ranges and needn't reach their ends.
Inputs may be any that keep to these rules, and one draw needn't show every extreme that they name: `lengths`: among the 2 clips c with the same c // 2, at least one has all 1024 frames live.
All inputs are finite; a program needn't handle non-finite values.
Results may differ from the reference program's by a relative error of at most 0.013.
Values may be sent and summed in bfloat16 or wider, within the bound.
No kernel may reach another device: no remote copies, remote signals or barrier semaphores. Data moves between devices by JAX's collectives and lax.ppermute only.
A program may use at most 192 MiB of HBM per device.

```python
import jax
import jax.numpy as jnp
from jax import lax

D = 768
FF = 3072
LEN = 1024
MICRO = 2
CLIPS = 16
LAYERS = 2


def draw_lengths(key, part):
    key = jax.random.fold_in(key, 7)
    first_key, second_key = jax.random.split(key)
    frames = jax.random.randint(first_key, (CLIPS,), LEN // 4, LEN + 1)
    chosen = jax.random.randint(second_key, (CLIPS // MICRO, 1), 0, MICRO)
    full = jnp.arange(MICRO)[None, :] == chosen
    return jnp.where(full, LEN, frames.reshape(CLIPS // MICRO, MICRO)).reshape(CLIPS).astype(jnp.int32)


def block_scale(rng, extent, shards, low, largest):
    factor_of = 1.0
    for position, shards_of in shards:
        heights = jax.random.uniform(jax.random.fold_in(jax.random.fold_in(rng, 6), position), (shards_of,), jnp.float32, low / len(shards), largest / len(shards))
        factor_of = factor_of * jnp.repeat(jnp.exp(heights), extent[position] // shards_of).reshape((-1,) + (1,) * (len(extent) - 1 - position))
    return factor_of


def normal_values(stream_key, extent, deviation, most, pieces=(), kind=jnp.bfloat16):
    factor_of = block_scale(stream_key, extent, pieces, -0.22, 0.18) if pieces else 1.0
    values = jax.random.normal(stream_key, extent, jnp.float32) * deviation * factor_of
    return jnp.minimum(jnp.maximum(values, -most), most).astype(kind)


def setup_inputs(seed: int = 0) -> dict:
    seeds = jax.random.split(jax.random.key(seed), 8)
    return {
        "ends_in": normal_values(seeds[0], (2, CLIPS, LEN, D), 1.0, 6.0, ((0, 2), (1, 8), (2, 2))),
        "lengths": draw_lengths(jax.random.fold_in(seeds[7], 71), 0),
        "vectors": normal_values(seeds[2], (LAYERS, 12, D), 0.3, 1.5, ((0, 2), (2, 16)), jnp.float32),
        "w_qkv": normal_values(seeds[3], (LAYERS, D, 3, D), D ** -0.5, 0.21875, ((0, 2), (1, 8), (3, 2))),
        "w_out": normal_values(seeds[4], (LAYERS, D, D), (D // 16) ** -0.5, 0.875, ((0, 2), (1, 2), (2, 8))),
        "w_up": normal_values(seeds[5], (LAYERS, D, FF), D ** -0.5, 0.21875, ((0, 2), (1, 8), (2, 2))),
        "w_down": normal_values(seeds[6], (LAYERS, FF, D), FF ** -0.5, 0.109375, ((0, 2), (1, 2), (2, 8))),
    }


@jax.custom_vjp
def low(v):
    return lax.optimization_barrier(v.astype(jnp.bfloat16)).astype(jnp.float32)

@jax.custom_vjp
def low_back(v):
    return v

def low_keep(v):
    return (low(v), None)

def low_pass(kept, grad):
    return (grad,)

def back_keep(v):
    return (v, None)

def back_low(kept, grad):
    return (low(grad),)
low.defvjp(low_keep, low_pass)
low_back.defvjp(back_keep, back_low)
HIGHEST = lax.Precision.HIGHEST

def layer_norm(values, gain, shift):
    centre = lax.optimization_barrier(jnp.mean(values, -1, keepdims=True))
    centred = values - centre
    spread = lax.optimization_barrier(jnp.mean(centred * centred, -1, keepdims=True))
    return centred * lax.rsqrt(spread + 1e-05) * (1.0 + gain) + shift

def encoder_layer(values, table, w_mixed, w_proj, w_rise, w_fall, mask):
    frames, width = values.shape
    heads = width // 64
    normed = low(layer_norm(values, table[0], table[1]))
    mixed_bias = jnp.stack([table[2], jnp.zeros_like(table[2]), table[3]])
    mixed = jnp.dot(normed, w_mixed.reshape(width, 3 * width), preferred_element_type=jnp.float32, precision=HIGHEST)
    mixed = low_back(low(mixed.reshape(frames, 3, width) + mixed_bias))
    query = mixed[:, 0].reshape(frames, heads, 64)
    keys = mixed[:, 1].reshape(frames, heads, 64)
    value = mixed[:, 2].reshape(frames, heads, 64)
    scores = low_back(jnp.einsum('qhd,khd->hqk', query, keys, precision=HIGHEST) * 0.125)
    scores = jnp.where(mask[None, None, :], scores, -1e+30)
    peak = lax.optimization_barrier(jnp.max(scores, -1, keepdims=True))
    raised = jnp.exp(scores - peak)
    weights = low(raised / lax.optimization_barrier(jnp.sum(raised, -1, keepdims=True)))
    attended = jnp.einsum('hqk,khd->qhd', weights, value, precision=HIGHEST).reshape(frames, width)
    attended = low_back(low(attended))
    branch = low_back(jnp.dot(attended, w_proj, preferred_element_type=jnp.float32, precision=HIGHEST))
    middle = values + branch + table[4]
    normed_two = low(layer_norm(middle, table[5], table[6]))
    before = jnp.dot(normed_two, w_rise, preferred_element_type=jnp.float32, precision=HIGHEST)
    before = low_back(before + table[8:12].reshape(-1))
    hidden = low(jax.nn.gelu(before, approximate=False))
    fall = low_back(jnp.dot(hidden, w_fall, preferred_element_type=jnp.float32, precision=HIGHEST))
    return middle + fall + table[7]

def reference(ends_in, lengths, vectors, w_qkv, w_out, w_up, w_down):
    inputs = ends_in[0].astype(jnp.float32)
    upstream = ends_in[1].astype(jnp.float32)
    params = (vectors.astype(jnp.float32), w_qkv.astype(jnp.float32), w_out.astype(jnp.float32), w_up.astype(jnp.float32), w_down.astype(jnp.float32))
    positions = jnp.arange(LEN)

    def per_clip(totals, item):
        clip, cotangent, frames = item
        mask = positions < frames

        def stacked(weights, values):
            for layer in range(LAYERS):
                values = encoder_layer(values, weights[0][layer], weights[1][layer], weights[2][layer], weights[3][layer], weights[4][layer], mask)
            return values
        output, pullback = jax.vjp(stacked, params, clip)
        grads, back = pullback(cotangent)
        totals = jax.tree.map(jnp.add, totals, grads)
        return (totals, (back, output))
    zeros = jax.tree.map(jnp.zeros_like, params)
    totals, (back, output) = lax.scan(per_clip, zeros, (inputs, upstream, lengths))
    return (jnp.stack([back, output]), totals[0], totals[1], totals[2], totals[3], totals[4])
```

```python
from functools import partial

import jax
import jax.numpy as jnp
from jax import lax
from jax.experimental import pallas as pl
from jax.experimental.pallas import tpu as pltpu
from jax.sharding import PartitionSpec as P

BF16 = jnp.bfloat16
F32 = jnp.float32
ROWS = (((0,), (0,)), ((), ()))
COLS = (((1,), (1,)), ((), ()))
PLAIN = (((1,), (0,)), ((), ()))
CROSS = ((0, 1), (1, 0))


def dot(left, right, dims=PLAIN):
    return lax.dot_general(left, right, dims, preferred_element_type=F32)


def swap(array, axis):
    return lax.ppermute(array, axis, CROSS)


def pair_swap(array, bit=1):
    return lax.ppermute(array, "dp", [(i, i ^ bit) for i in range(lax.axis_size("dp"))])


def ring_shift(array, by):
    ring = lax.axis_size("dp") // 2
    pairs = [(2 * z + x, 2 * ((z + by) % ring) + x) for z in range(ring) for x in (0, 1)]
    return lax.ppermute(array, "dp", pairs)


def added(left, right, kind=BF16):
    return (left.astype(F32) + right.astype(F32)).astype(kind)


class Line:
    def __init__(self, steps):
        self.steps, self.result, self.done = steps, None, False
        self.pending = next(steps)

    def advance(self, arrays):
        try:
            self.pending = self.steps.send(arrays)
        except StopIteration as end:
            self.result, self.done, self.pending = end.value, True, ()


def join(state, *lines):
    lines = [line for line in lines if not line.done]
    state, arrays = lax.optimization_barrier((state, [tuple(line.pending) for line in lines]))
    for line, own in zip(lines, arrays):
        line.advance(own)
    return state


def ring_gather(piece):
    ring = lax.axis_size("dp") // 2
    if ring <= 4:
        pieces = [piece]
        for _ in range(ring - 1):
            (piece,) = yield (ring_shift(pieces[-1], 1),)
            pieces.append(piece)
        return jnp.stack(pieces)

    def step(k, state):
        moving, held = state
        moving = ring_shift(moving, 1)
        return moving, lax.dynamic_update_index_in_dim(held, moving, k, 0)

    held = jnp.zeros((ring,) + piece.shape, piece.dtype).at[0].set(piece)
    return lax.fori_loop(1, ring, step, (piece, held))[1]


def ring_scatter(parts):
    ring = lax.axis_size("dp") // 2
    if ring <= 4:
        total = parts[ring - 1]
        for k in reversed(range(ring - 1)):
            (came,) = yield (ring_shift(total.astype(BF16), -1),)
            total = parts[k] + came.astype(F32)
        return total

    def step(k, total):
        mine = lax.dynamic_index_in_dim(parts, ring - 1 - k, 0, keepdims=False)
        return mine + ring_shift(total.astype(BF16), -1).astype(F32)

    return lax.fori_loop(1, ring, step, parts[ring - 1])


def copy_kernel(plan, count, *refs):
    sources, outs, sems = refs[:count], refs[count:-1], refs[-1]
    copies = []
    for source, (out, row) in zip(sources, plan):
        copies.append(
            pltpu.make_async_copy(
                source, outs[out].at[pl.ds(row, source.shape[0])], sems.at[len(copies)]
            )
        )
    for copy in copies:
        copy.start()
    for copy in copies:
        copy.wait()


def stack_rows(*groups):
    sources = [part for group in groups for part in group]
    plan, outs = [], []
    for index, group in enumerate(groups):
        row = 0
        for part in group:
            plan.append((index, row))
            row += part.shape[0]
        outs.append(jax.ShapeDtypeStruct((row,) + group[0].shape[1:], group[0].dtype))
    return pl.pallas_call(
        partial(copy_kernel, plan, len(sources)),
        out_shape=outs,
        in_specs=[pl.BlockSpec(memory_space=pl.ANY)] * len(sources),
        out_specs=[pl.BlockSpec(memory_space=pltpu.VMEM)] * len(outs),
        scratch_shapes=[pltpu.SemaphoreType.DMA((len(sources),))],
        compiler_params=pltpu.CompilerParams(vmem_limit_bytes=24 * 1024 * 1024),
        cost_estimate=pl.CostEstimate(
            flops=0, bytes_accessed=sum(4 * part.size for part in sources), transcendentals=0
        ),
        name="stack_rows",
    )(*sources)


def gather_chunk(piece):
    columns = piece.shape[1]
    ring = lax.axis_size("dp") // 2
    half = ring // 2
    near = yield from ring_gather(piece)
    over_x, over_y = yield (pair_swap(near), swap(near, "tensor"))
    first, second = yield (swap(over_x[:half], "tensor"), pair_swap(over_y[half:]))
    flat = lambda part: part.reshape(-1, columns)
    if piece.shape[0] % 16 == 0:
        mine = stack_rows([near, over_x, over_y, first, second])[0]
        mine = mine.reshape(2, -1, columns)
        (theirs,) = yield (swap(mine, "section"),)
        return stack_rows([mine[0], theirs[0]], [mine[1], theirs[1]])
    mine = jnp.concatenate([near, over_x, over_y, first, second]).reshape(2, -1, columns)
    (theirs,) = yield (swap(mine, "section"),)
    return [jnp.concatenate([mine[t], theirs[t]]) for t in (0, 1)]


def scatter_chunk(own, other):
    ring = lax.axis_size("dp") // 2
    half = ring // 2
    columns = own[0].shape[1]
    rows = own[0].shape[0] // (2 * ring)
    came = yield tuple(swap(part, "section") for part in other)
    quarter = ring * rows

    def part(dx, dy, low, high, kind):
        cut = slice(dx * quarter + low * rows, dx * quarter + high * rows)
        return added(own[dy][cut], came[dy][cut], kind).reshape(high - low, rows, columns)

    first, second = yield (
        swap(part(1, 1, 0, half, BF16), "tensor"),
        pair_swap(part(1, 1, half, ring, BF16)),
    )
    over_x = jnp.concatenate(
        [added(part(1, 0, 0, half, F32), first), part(1, 0, half, ring, BF16)]
    )
    over_y = jnp.concatenate(
        [part(0, 1, 0, half, BF16), added(part(0, 1, half, ring, F32), second)]
    )
    over_x, over_y = yield (pair_swap(over_x), swap(over_y, "tensor"))
    near = part(0, 0, 0, ring, F32) + over_x.astype(F32) + over_y.astype(F32)
    total = yield from ring_scatter(near)
    return total


def finish(line):
    while not line.done:
        join((), line)
    return line.result


def attend_kernel(scale, q_ref, k0_ref, k1_ref, v0_ref, v1_ref, b0_ref, b1_ref, o_ref, lse_ref):
    span = q_ref.shape[0]
    lane = lax.broadcasted_iota(jnp.int32, (span, 128), 1)
    q = q_ref[...]
    k0, k1 = k0_ref[...], k1_ref[...]
    v0, v1 = v0_ref[...], v1_ref[...]
    b0, b1 = b0_ref[...], b1_ref[...]
    outs = []
    for head in (0, 1):
        own = (lane >= 64 * head) & (lane < 64 * head + 64)
        qh = jnp.where(own, q * jnp.asarray(scale, BF16), jnp.zeros_like(q))
        s0 = dot(k0, qh, COLS) + b0
        s1 = dot(k1, qh, COLS) + b1
        peak = jnp.maximum(jnp.max(s0, 0, keepdims=True), jnp.max(s1, 0, keepdims=True))
        p0 = jnp.exp(s0 - peak)
        p1 = jnp.exp(s1 - peak)
        total = jnp.sum(p0, 0, keepdims=True) + jnp.sum(p1, 0, keepdims=True)
        out = dot(v0, p0.astype(BF16), ROWS) + dot(v1, p1.astype(BF16), ROWS)
        outs.append(out / total)
        lse_ref[0, head : head + 1, :] = peak + jnp.log(total)
    row = lax.broadcasted_iota(jnp.int32, (128, span), 0)
    o_ref[...] = jnp.where(row < 64, outs[0], outs[1]).T.astype(BF16)


def attend(mixed, other, biases):
    span, width = mixed.shape
    groups = width // (3 * 128)
    block = lambda first: pl.BlockSpec((span, 128), lambda g, first=first: (0, first * groups + g))
    bias = pl.BlockSpec((span, 1), lambda g: (0, 0))
    return pl.pallas_call(
        partial(attend_kernel, 0.125),
        grid=(groups,),
        out_shape=[
            jax.ShapeDtypeStruct((span, width // 3), BF16),
            jax.ShapeDtypeStruct((groups, 8, span), F32),
        ],
        in_specs=[block(0), block(1), block(0), block(2), block(1), bias, bias],
        out_specs=[block(0), pl.BlockSpec((1, 8, span), lambda g: (g, 0, 0))],
        compiler_params=pltpu.CompilerParams(vmem_limit_bytes=48 * 1024 * 1024),
        cost_estimate=pl.CostEstimate(
            flops=16 * groups * span * span * 2 * 128,
            bytes_accessed=8 * span * width,
            transcendentals=4 * groups * span * span,
        ),
        name="attend",
    )(mixed, mixed, other, mixed, other, *biases)


def attend_back_kernel(
    scale, q_ref, k0_ref, k1_ref, v0_ref, v1_ref, b0_ref, b1_ref, lse_ref, do_ref,
    dq_ref, dk0_ref, dk1_ref, dv0_ref, dv1_ref,
):
    span = q_ref.shape[0]
    lane = lax.broadcasted_iota(jnp.int32, (span, 128), 1)
    q, above = q_ref[...], do_ref[...]
    keys = (k0_ref[...], k1_ref[...])
    values = (v0_ref[...], v1_ref[...])
    biases = (b0_ref[...], b1_ref[...])
    dqs, dks, dvs = [], [], []
    for head in (0, 1):
        own = (lane >= 64 * head) & (lane < 64 * head + 64)
        qh = jnp.where(own, q * jnp.asarray(scale, BF16), jnp.zeros_like(q))
        ah = jnp.where(own, above, jnp.zeros_like(above))
        lse = lse_ref[0, head : head + 1, :]
        probs, pushed = [], []
        for part in (0, 1):
            probs.append(jnp.exp(dot(keys[part], qh, COLS) + biases[part] - lse))
            pushed.append(dot(values[part], ah, COLS))
        inner = jnp.sum(probs[0] * pushed[0], 0, keepdims=True) + jnp.sum(
            probs[1] * pushed[1], 0, keepdims=True
        )
        dq = None
        for part in (0, 1):
            slopes = (probs[part] * (pushed[part] - inner)).astype(BF16)
            piece = dot(keys[part], slopes, ROWS)
            dq = piece if dq is None else dq + piece
            dk = dot(slopes, qh)
            dv = dot(probs[part].astype(BF16), ah)
            if head == 0:
                dks.append(dk)
                dvs.append(dv)
            else:
                dks[part] = dks[part] + dk
                dvs[part] = dvs[part] + dv
        dqs.append(dq)
    row = lax.broadcasted_iota(jnp.int32, (128, span), 0)
    dq_ref[...] = (jnp.where(row < 64, dqs[0], dqs[1]) * scale).T.astype(BF16)
    dk0_ref[...] = dks[0].astype(BF16)
    dk1_ref[...] = dks[1].astype(BF16)
    dv0_ref[...] = dvs[0].astype(BF16)
    dv1_ref[...] = dvs[1].astype(BF16)


def attend_back(mixed, other, biases, lse, above):
    span, width = mixed.shape
    groups = width // (3 * 128)
    block = lambda first: pl.BlockSpec((span, 128), lambda g, first=first: (0, first * groups + g))
    bias = pl.BlockSpec((span, 1), lambda g: (0, 0))
    out = jax.ShapeDtypeStruct((span, width // 3), BF16)
    return pl.pallas_call(
        partial(attend_back_kernel, 0.125),
        grid=(groups,),
        out_shape=[out] * 5,
        in_specs=[block(0), block(1), block(0), block(2), block(1), bias, bias]
        + [pl.BlockSpec((1, 8, span), lambda g: (g, 0, 0)), block(0)],
        out_specs=[block(0)] * 5,
        compiler_params=pltpu.CompilerParams(vmem_limit_bytes=56 * 1024 * 1024),
        cost_estimate=pl.CostEstimate(
            flops=40 * groups * span * span * 2 * 128,
            bytes_accessed=12 * span * width,
            transcendentals=4 * groups * span * span,
        ),
        name="attend_back",
    )(mixed, mixed, other, mixed, other, *biases, lse, above)


def layer_norm(values, gain, shift):
    centre = jnp.mean(values, -1, keepdims=True)
    centred = values - centre
    spread = jnp.mean(centred * centred, -1, keepdims=True)
    return centred * lax.rsqrt(spread + 1e-05) * (1.0 + gain) + shift


def attention_forward(values, w_a, table, biases):
    third = w_a[0].shape[-1] // 4
    normed = layer_norm(values, table[0], table[1]).astype(BF16)
    mixed, other = [], []
    for t in (0, 1):
        cut = slice(t * third, (t + 1) * third)
        bias = jnp.concatenate([table[2, cut], jnp.zeros((third,), F32), table[3, cut]])
        mixed.append((dot(normed, w_a[t][:, : 3 * third]) + bias).astype(BF16))
        other.append(swap(mixed[t][:, third:], "section"))
    attended, logs = [], []
    for t in (0, 1):
        o, lse = attend(mixed[t], other[t], biases)
        attended.append(o)
        logs.append(lse)
    return normed, mixed, other, attended, logs


def middle_forward(values, attended, w_a, table):
    third = w_a[0].shape[-1] // 4
    branch = sum(dot(attended[t], w_a[t][:, 3 * third :], COLS) for t in (0, 1))
    middle = values + branch + table[4]
    return middle, layer_norm(middle, table[5], table[6]).astype(BF16)


def hidden_forward(normed_two, w_b, table):
    rise = table[8:12].reshape(2, -1)
    hidden, slope = [], []
    for t in (0, 1):
        before = dot(normed_two, w_b[t]) + rise[t]
        share = 0.5 * (1.0 + lax.erf(before * (0.5**0.5)))
        hidden.append((before * share).astype(BF16))
        bell = jnp.exp(-0.5 * before * before) * 0.3989422804014327
        slope.append((share + before * bell).astype(BF16))
    return hidden, slope


def hidden_down(middle, hidden, w_c, table):
    return middle + sum(dot(hidden[t], w_c[t], COLS) for t in (0, 1)) + table[7]


def by_core(left, rights):
    half = left.shape[1] // 2
    return [
        [dot(left[:, cut], right, ROWS).astype(BF16) for right in rights]
        for cut in (slice(0, half), slice(half, None))
    ]


def hidden_back(incoming, w_c, slope):
    short = incoming.astype(BF16)
    return [(dot(short, w_c[t]) * slope[t].astype(F32)).astype(BF16) for t in (0, 1)]


def middle_back(incoming, pushed, middle, w_a, w_b, table):
    third = w_a[0].shape[-1] // 4
    grad_normed = sum(dot(pushed[t], w_b[t], COLS) for t in (0, 1))
    _, back = jax.vjp(layer_norm, middle, table[5], table[6])
    grad_mid, gain, shift = back(grad_normed)
    grad_middle = incoming + grad_mid
    proj_in = grad_middle.astype(BF16)
    above = [dot(proj_in, w_a[t][:, 3 * third :]).astype(BF16) for t in (0, 1)]
    return grad_middle, proj_in, above, gain, shift


def input_back(grad_middle, flats, values, w_a, table):
    third = w_a[0].shape[-1] // 4
    grad_normed = sum(dot(flats[t], w_a[t][:, : 3 * third], COLS) for t in (0, 1))
    _, back = jax.vjp(layer_norm, values, table[0], table[1])
    grad_input, gain, shift = back(grad_normed)
    return grad_middle + grad_input, gain, shift


def table_back(incoming, pushed, grad_middle, flats, gains):
    third = flats[0].shape[1] // 3
    sums = [jnp.sum(flat, 0, dtype=F32) for flat in flats]
    rows = [
        gains[0],
        gains[1],
        jnp.concatenate([part[:third] for part in sums]),
        jnp.concatenate([part[2 * third :] for part in sums]),
        jnp.sum(grad_middle, 0),
        gains[2],
        gains[3],
        jnp.sum(incoming, 0),
    ]
    rise = jnp.concatenate([jnp.sum(part, 0, dtype=F32) for part in pushed]).reshape(4, -1)
    return jnp.concatenate([jnp.stack(rows), rise])


def attention_back(mixed, other, biases, logs, above):
    dq, dk, dk_far, dv, dv_far = attend_back(mixed, other, biases, logs, above)
    far = swap(jnp.concatenate([dk_far, dv_far], 1), "section")
    return dq, jnp.concatenate([dk, dv], 1), far


def far_back(parts):
    query, near, far = parts
    return jnp.concatenate([query, added(near, far)], 1)


def beside(left, right):
    return [[jnp.concatenate(pair, 1) for pair in zip(*sides)] for sides in zip(left, right)]


def iter_swaps(rows, first, side, core):
    span, width = rows.shape
    (came,) = yield (lax.ppermute(rows.astype(BF16), "section", [(1 - core, core)]),)
    came = came.astype(F32)
    full = jnp.stack([rows, came] if core == 0 else [came, rows])
    keep = lax.dynamic_index_in_dim(full, side, 0, keepdims=False)
    gone = lax.dynamic_index_in_dim(full, 1 - side, 0, keepdims=False).astype(BF16)
    pairs = [(2 * core, 2 * core + 1), (2 * core + 1, 2 * core)]
    (came,) = yield (lax.ppermute(gone, ("section", "tensor"), pairs),)
    came = came.astype(F32)
    return jnp.where(side == 0, jnp.stack([keep, came]), jnp.stack([came, keep]))


def iter_tables(tables, count):
    (came,) = yield (swap(tables, "section"),)
    tables = tables + came
    (came,) = yield (swap(tables, "tensor"),)
    tables = tables + came
    bit = 1
    while bit < count:
        (came,) = yield (pair_swap(tables, bit),)
        tables = tables + came
        bit *= 2
    return tables


FEATURE_ROWS = (True, True, False, False, True, True, True, True, False, False, False, False)


def body(ends_in, lengths, vectors, w_qkv, w_out, w_up, w_down):
    core = lax.axis_index("section")
    first = core == 0
    side = lax.axis_index("tensor")
    count = lax.axis_size("dp")
    ring = count // 2
    rows = w_qkv.shape[1]
    half = rows // 2
    span, width = ends_in.shape[2:]
    third, unit = w_qkv.shape[-1], w_up.shape[-1]

    at = jnp.arange(width, dtype=jnp.int32)
    row, rest = at % half, at // half
    step, rest = rest % ring, rest // ring
    spot = lax.axis_index("dp")
    owner = 2 * ((spot // 2 - step + ring) % ring) + (spot % 2 + rest % 2) % 2
    source = owner * rows + ((core + rest // 2) % 2) * half + row
    order = at[:, None] == source[None, :]
    order_low = order.astype(BF16)

    def to_own(array):
        return jnp.dot(array, order.astype(F32), precision=lax.Precision.HIGHEST)

    def from_own(array):
        return lax.dot_general(array, order.astype(F32), COLS, precision=lax.Precision.HIGHEST)

    keep = lax.dynamic_index_in_dim(ends_in[0], side, 0, keepdims=False)
    gone = lax.dynamic_index_in_dim(ends_in[0], 1 - side, 0, keepdims=False)
    came = swap(gone, "tensor")
    upper, lower = jnp.where(side == 0, keep, came), jnp.where(side == 0, came, keep)
    stay, leave = jnp.where(first, upper, lower), jnp.where(first, lower, upper)
    came = swap(leave, "section")
    values = dot(jnp.where(first, stay, came), order_low)
    upstream = dot(jnp.where(first, came, stay), order_low)
    frames = lax.dynamic_index_in_dim(lengths, side, 0, keepdims=False)
    spots = lax.broadcasted_iota(jnp.int32, (span, 1), 0)
    biases = [
        jnp.where(spots + offset * span < frames, 0.0, -1e30).astype(F32)
        for offset in (core, 1 - core)
    ]

    index = spot * 2 + side
    cut = vectors.shape[-1]
    spread = lax.dynamic_update_slice_in_dim(
        jnp.zeros((vectors.shape[1], width), F32), vectors[0], index * cut, 1
    )
    spread = spread + swap(spread, "tensor")
    bit = 1
    while bit < count:
        spread = spread + pair_swap(spread, bit)
        bit *= 2
    theirs = swap(spread, "section")
    is_feature = jnp.array(FEATURE_ROWS)[:, None]

    def own_table(table):
        heads = jnp.roll(table[:8].reshape(8, 2, -1), side, 1).reshape(8, width)
        rise = jnp.roll(table[8:].reshape(2, 2, width), side, 0).reshape(4, width)
        return jnp.where(is_feature, to_own(table), jnp.concatenate([heads, rise]))

    def plain_table(table):
        heads = jnp.roll(table[:8].reshape(8, 2, -1), side, 1).reshape(8, width)
        rise = jnp.roll(table[8:].reshape(2, 2, width), side, 0).reshape(4, width)
        return jnp.where(is_feature, from_own(table), jnp.concatenate([heads, rise]))

    tables = [
        own_table(jnp.where(first, spread, theirs)),
        own_table(jnp.where(first, theirs, spread)),
    ]

    own = jnp.concatenate([w_qkv[0].reshape(rows, -1), w_out[0].T, w_up[0], w_down[0].T], 1)
    halves = (own[:half], own[half:])
    came = swap(jnp.where(first, halves[1], halves[0]), "section")
    one, two = jnp.where(first, halves[0], came), jnp.where(first, came, halves[1])
    cuts = [slice(n * unit, (n + 1) * unit) for n in range(3)]
    chunks = [layer[:, c] for layer in (one, two) for c in cuts]

    a0 = Line(gather_chunk(chunks[0]))
    join((), a0)
    join((), a0)
    ready = join(chunks[1], a0)
    b0 = Line(gather_chunk(ready))
    join((), b0)
    join((), b0)
    ready, *_ = join((chunks[2],), a0, b0)
    c0 = Line(gather_chunk(ready))
    join((), c0)
    join((), c0)
    (ready,) = join((chunks[3],), a0, b0, c0)
    a1 = Line(gather_chunk(ready))
    join((), a0)
    w_a0 = a0.result
    normed_0, mixed_0, other_0, attended_0, logs_0 = attention_forward(
        values, w_a0, tables[0], biases
    )
    join((), a1)
    join((), a1)
    attended_0, ready = join((attended_0, chunks[4]), b0, c0, a1)
    b1 = Line(gather_chunk(ready))
    middle_0, short_0 = middle_forward(values, attended_0, w_a0, tables[0])
    short_0 = join(short_0, b0)
    w_b0 = b0.result
    hidden_0, slope_0 = hidden_forward(short_0, w_b0, tables[0])
    join((), b1)
    join((), b1)
    hidden_0, slope_0, ready = join((hidden_0, slope_0, chunks[5]), c0, a1, b1)
    c1 = Line(gather_chunk(ready))
    hidden_0 = join(hidden_0, c0)
    w_c0 = c0.result
    layer_one = hidden_down(middle_0, hidden_0, w_c0, tables[0])
    join((), c1)
    join((), c1)
    layer_one = join(layer_one, a1, b1, c1)
    layer_one = join(layer_one, a1)
    w_a1 = a1.result
    normed_1, mixed_1, other_1, attended_1, logs_1 = attention_forward(
        layer_one, w_a1, tables[1], biases
    )
    attended_1 = join(attended_1, b1, c1)
    middle_1, short_1 = middle_forward(layer_one, attended_1, w_a1, tables[1])
    short_1 = join(short_1, b1)
    w_b1 = b1.result
    hidden_1, slope_1 = hidden_forward(short_1, w_b1, tables[1])
    grad_c = by_core(upstream.astype(BF16), hidden_1)
    grad_c = join(grad_c, c1)
    sc1 = Line(scatter_chunk(*grad_c))
    w_c1 = finish(c1)
    result = hidden_down(middle_1, hidden_1, w_c1, tables[1])
    result = from_own(result)
    pushed_1 = hidden_back(upstream, w_c1, slope_1)
    pushed_1 = join(pushed_1, sc1)

    out = Line(iter_swaps(result, first, side, 1))
    grad_b = by_core(short_1, pushed_1)
    grad_mid_1, proj_1, above_1, gain_1, shift_1 = middle_back(
        upstream, pushed_1, middle_1, w_a1, w_b1, tables[1]
    )
    grad_o = by_core(proj_1, attended_1)
    grad_b, grad_o, above_1 = join((grad_b, grad_o, above_1), sc1, out)
    sb1 = Line(scatter_chunk(*beside(grad_b, grad_o)))
    flat_a = attention_back(mixed_1[0], other_1[0], biases, logs_1[0], above_1[0])
    flat_a, up = join((flat_a, above_1[1]), sc1, sb1)
    flat_b = attention_back(mixed_1[1], other_1[1], biases, logs_1[1], up)
    flat_a = far_back(flat_a)
    flat_a, flat_b = join((flat_a, flat_b), sc1, sb1, out)
    flats_1 = [flat_a, far_back(flat_b)]
    grad_q = by_core(normed_1, flats_1)
    grad_q, flats_1 = join((grad_q, flats_1), sc1)
    sq1 = Line(scatter_chunk(*grad_q))
    grad_layer, gain_1a, shift_1a = input_back(grad_mid_1, flats_1, layer_one, w_a1, tables[1])
    grad_layer = join(grad_layer, sc1, sb1, sq1)
    table_1 = table_back(upstream, pushed_1, grad_mid_1, flats_1, (gain_1a, shift_1a, gain_1, shift_1))

    grad_c = by_core(grad_layer.astype(BF16), hidden_0)
    grad_c = join(grad_c, sb1, sq1)
    sc0 = Line(scatter_chunk(*grad_c))
    pushed_0 = hidden_back(grad_layer, w_c0, slope_0)
    pushed_0 = join(pushed_0, sc0, sb1)
    grad_b = by_core(short_0, pushed_0)
    grad_mid_0, proj_0, above_0, gain_0, shift_0 = middle_back(
        grad_layer, pushed_0, middle_0, w_a0, w_b0, tables[0]
    )
    grad_o = by_core(proj_0, attended_0)
    grad_b, grad_o, above_0 = join((grad_b, grad_o, above_0), sc0, sq1, sb1)
    sb0 = Line(scatter_chunk(*beside(grad_b, grad_o)))
    flat_a = attention_back(mixed_0[0], other_0[0], biases, logs_0[0], above_0[0])
    flat_a, up = join((flat_a, above_0[1]), sc0, sb0, sq1)
    flat_b = attention_back(mixed_0[1], other_0[1], biases, logs_0[1], up)
    flat_a = far_back(flat_a)
    flat_a, flat_b = join((flat_a, flat_b), sc0, sb0, sq1)
    flats_0 = [flat_a, far_back(flat_b)]
    grad_q = by_core(normed_0, flats_0)
    grad_q, flats_0 = join((grad_q, flats_0), sc0)
    sq0 = Line(scatter_chunk(*grad_q))
    grad_values, gain_0a, shift_0a = input_back(grad_mid_0, flats_0, values, w_a0, tables[0])
    table_0 = table_back(grad_layer, pushed_0, grad_mid_0, flats_0, (gain_0a, shift_0a, gain_0, shift_0))
    grad_values = from_own(grad_values)
    grad_values = join(grad_values, sc0, sb0, sq0)
    into = Line(iter_swaps(grad_values, first, side, 0))
    tables_back = Line(iter_tables(jnp.stack([plain_table(table_0), plain_table(table_1)]), count))
    join((), into, tables_back, sq0, sb0)
    lines = [into, out, tables_back, sq0, sb0, sc0, sq1, sb1, sc1]
    while any(not line.done for line in lines):
        join((), *lines)

    boundary = jnp.where(first, into.result, out.result)

    sums_one = (sq0.result, sb0.result, sc0.result)
    sums_two = (sq1.result, sb1.result, sc1.result)
    grads = []
    for one, two in zip(sums_one, sums_two):
        lower = lax.ppermute(one.astype(BF16), "section", [(1, 0)]).astype(F32)
        upper = lax.ppermute(two.astype(BF16), "section", [(0, 1)]).astype(F32)
        grads.append(
            jnp.where(first, jnp.concatenate([one, lower]), jnp.concatenate([upper, two]))
        )
    table_grad = lax.dynamic_index_in_dim(tables_back.result, core, 0, keepdims=False)
    table_grad = lax.dynamic_slice_in_dim(table_grad, index * cut, cut, 1)
    return (
        boundary[None],
        table_grad[None],
        grads[0].reshape(w_qkv.shape),
        grads[1][:, unit:].T[None],
        grads[1][None, :, :unit],
        grads[2].T[None],
    )


def solution(mesh):
    in_specs = (
        P("section", "dp", "tensor", None),
        P("dp"),
        P("section", None, ("dp", "tensor")),
        P("section", "dp", None, "tensor"),
        P("section", "tensor", "dp"),
        P("section", "dp", "tensor"),
        P("section", "tensor", "dp"),
    )
    out_specs = (
        P("section", "dp", "tensor", None),
        P("section", None, ("dp", "tensor")),
        P("section", "dp", None, "tensor"),
        P("section", "tensor", "dp"),
        P("section", "dp", "tensor"),
        P("section", "tensor", "dp"),
    )
    return jax.shard_map(body, mesh=mesh, in_specs=in_specs, out_specs=out_specs, check_vma=False)
```

```python
from functools import partial

import jax
import jax.numpy as jnp
from jax import lax
from jax.experimental import pallas as pl
from jax.experimental.pallas import tpu as pltpu
from jax.sharding import PartitionSpec as P

BF16 = jnp.bfloat16
F32 = jnp.float32
ROWS = (((0,), (0,)), ((), ()))
COLS = (((1,), (1,)), ((), ()))
PLAIN = (((1,), (0,)), ((), ()))
CROSS = ((0, 1), (1, 0))


def cost(flops, size, exps=0):
    return pl.CostEstimate(flops=flops, bytes_accessed=size, transcendentals=exps)


def dot(left, right, dims=PLAIN):
    return lax.dot_general(left, right, dims, preferred_element_type=F32)


def swap(array, axis):
    return lax.ppermute(array, axis, CROSS)


def pair_swap(array, bit=1):
    return lax.ppermute(array, "dp", [(i, i ^ bit) for i in range(lax.axis_size("dp"))])


def ring_shift(array, by):
    ring = lax.axis_size("dp") // 2
    pairs = [(2 * z + x, 2 * ((z + by) % ring) + x) for z in range(ring) for x in (0, 1)]
    return lax.ppermute(array, "dp", pairs)


def tied(state, after):
    return lax.optimization_barrier((state, after))[0] if after else state


class Line:
    def __init__(self, steps, after=()):
        self.steps, self.result, self.done = steps, None, False
        self.take(next(steps), after)

    def take(self, step, after):
        self.sent = tied([array for _, array in step], after)
        self.pending = [send(array) for (send, _), array in zip(step, self.sent)]

    def advance(self, arrays, after):
        try:
            self.take(self.steps.send(arrays), after)
        except StopIteration as end:
            self.result, self.done, self.pending, self.sent = end.value, True, [], []


def join(state, *lines):
    lines = [line for line in lines if not line.done]
    state, arrays = lax.optimization_barrier((state, [line.pending for line in lines]))
    sent = []
    for line, own in zip(lines, arrays):
        line.advance(own, sent)
        sent = sent + line.sent
    return tied(state, sent)


def over(axis):
    return lambda array: swap(array, axis)


def around(by):
    return lambda array: ring_shift(array, by)


def ring_gather(piece):
    ring = lax.axis_size("dp") // 2
    if ring <= 4:
        came = yield [(around(k), piece) for k in range(1, ring)]
        return [piece, *came]

    def step(k, state):
        moving, held = state
        moving = ring_shift(moving, 1)
        return moving, lax.dynamic_update_index_in_dim(held, moving, k, 0)

    held = jnp.zeros((ring,) + piece.shape, piece.dtype).at[0].set(piece)
    held = lax.fori_loop(1, ring, step, (piece, held))[1]
    return [held.reshape(-1, piece.shape[1])]


def ring_scatter(parts):
    ring = len(parts)
    if ring <= 4:
        came = yield [(around(-k), parts[k]) for k in range(1, ring)]
        return sum((part.astype(F32) for part in came), parts[0])

    stacked = jnp.stack([part.astype(BF16) for part in parts[1:]])

    def step(k, total):
        mine = lax.dynamic_index_in_dim(stacked, ring - 2 - k, 0, keepdims=False)
        return mine.astype(F32) + ring_shift(total.astype(BF16), -1).astype(F32)

    total = lax.fori_loop(1, ring - 1, step, stacked[ring - 2].astype(F32))
    return parts[0] + ring_shift(total.astype(BF16), -1).astype(F32)


def copy_kernel(plan, count, *refs):
    sources, outs, sems = refs[:count], refs[count:-1], refs[-1]
    copies = []
    for source, (out, row) in zip(sources, plan):
        copies.append(
            pltpu.make_async_copy(
                source, outs[out].at[pl.ds(row, source.shape[0])], sems.at[len(copies)]
            )
        )
    for copy in copies:
        copy.start()
    for copy in copies:
        copy.wait()


def stack_rows(*groups):
    sources = [part for group in groups for part in group]
    plan, outs = [], []
    for index, group in enumerate(groups):
        row = 0
        for part in group:
            plan.append((index, row))
            row += part.shape[0]
        outs.append(jax.ShapeDtypeStruct((row,) + group[0].shape[1:], group[0].dtype))
    return pl.pallas_call(
        partial(copy_kernel, plan, len(sources)),
        out_shape=outs,
        in_specs=[pl.BlockSpec(memory_space=pl.ANY)] * len(sources),
        out_specs=[pl.BlockSpec(memory_space=pltpu.VMEM)] * len(outs),
        scratch_shapes=[pltpu.SemaphoreType.DMA((len(sources),))],
        compiler_params=pltpu.CompilerParams(vmem_limit_bytes=(1 << 20) + sum(2 * out.size for out in outs)),
        cost_estimate=cost(0, sum(4 * part.size for part in sources)),
        name="stack_rows",
    )(*sources)


def gather_chunk(piece):
    rows, columns = piece.shape
    low = (lax.axis_size("dp") // 4) * rows
    near = yield from ring_gather(piece)
    near = stack_rows(near)[0] if len(near) > 1 and rows % 16 == 0 else jnp.concatenate(near)
    over_x, over_y = yield [(pair_swap, near), (over("tensor"), near)]
    first, second = yield [(over("tensor"), over_x[:low]), (pair_swap, over_y[low:])]
    mine = stack_rows([near, over_x, over_y, first, second])[0]
    mine = mine.reshape(2, -1, columns)
    (theirs,) = yield [(over("section"), mine)]
    return stack_rows([mine[0], theirs[0]], [mine[1], theirs[1]])


def pick_kernel(ring, column, place, mine, theirs, out0, out1, sems):
    z, x, y = place[0], place[1], place[2]
    rows, columns = mine.shape[1], out0.shape[1]
    copies = []
    for ds, source in enumerate((mine, theirs)):
        for dx in (0, 1):
            for k in range(ring):
                owner = 2 * lax.rem(z - k + ring, ring) + (x + dx) % 2
                row = ((ds * 2 + dx) * ring + k) * rows
                for dy, out in enumerate((out0, out1)):
                    copies.append(
                        pltpu.make_async_copy(
                            source.at[2 * owner + (y + dy) % 2, :, pl.ds(column, columns)],
                            out.at[pl.ds(row, rows)],
                            sems.at[len(copies)],
                        )
                    )
    for copy in copies:
        copy.start()
    for copy in copies:
        copy.wait()


def pick(place, mine, theirs, column, columns):
    groups, rows, _ = mine.shape
    ring = groups // 4
    if rows % 16:
        return pick_plain(place, mine, theirs, column, columns)
    out = like((groups * rows, columns))
    return pl.pallas_call(
        partial(pick_kernel, ring, column),
        out_shape=[out, out],
        in_specs=[pl.BlockSpec(memory_space=pltpu.SMEM)] + [pl.BlockSpec(memory_space=pl.ANY)] * 2,
        out_specs=[pl.BlockSpec(memory_space=pltpu.VMEM)] * 2,
        scratch_shapes=[pltpu.SemaphoreType.DMA((2 * groups,))],
        compiler_params=pltpu.CompilerParams(vmem_limit_bytes=6 * 1024 * 1024),
        cost_estimate=cost(0, 4 * groups * rows * columns),
        name="pick",
    )(place, mine, theirs)


def pick_plain(place, mine, theirs, column, columns):
    groups, rows, _ = mine.shape
    ring = groups // 4
    near = jnp.arange(groups // 2) % ring
    owner = 2 * ((place[0] - near + ring) % ring) + (place[1] + jnp.arange(groups // 2) // ring) % 2
    outs = []
    for dy in (0, 1):
        which = 2 * owner + (place[2] + dy) % 2
        parts = [part[:, :, column : column + columns][which] for part in (mine, theirs)]
        outs.append(jnp.concatenate(parts).reshape(-1, columns))
    return outs


def total_of(own, came):
    return own[0].astype(F32) + came[0].astype(F32)


def corner_kernel(low, own, came, first, second):
    total = total_of(own, came)
    first[...] = total[:low].astype(BF16)
    second[...] = total[low:].astype(BF16)


def sides_kernel(low, own_x, came_x, own_y, came_y, first, second, over_x, over_y):
    total = total_of(own_x, came_x)
    over_x[:low] = (total[:low] + first[...].astype(F32)).astype(BF16)
    over_x[low:] = total[low:].astype(BF16)
    total = total_of(own_y, came_y)
    over_y[:low] = total[:low].astype(BF16)
    over_y[low:] = (total[low:] + second[...].astype(F32)).astype(BF16)


def near_kernel(own, came, over_x, over_y, *near):
    total = total_of(own, came) + over_x[...].astype(F32) + over_y[...].astype(F32)
    rows = near[0].shape[0]
    for k, out in enumerate(near):
        out[...] = total[k * rows : (k + 1) * rows].astype(out.dtype)


def call(kernel, name, ins, outs, flops=0, exps=0, limit=5, specs=None, aliases=None):
    size = lambda a: a.size * a.dtype.itemsize
    return pl.pallas_call(
        kernel,
        out_shape=outs,
        in_specs=specs or [pl.BlockSpec(memory_space=pltpu.VMEM)] * len(ins),
        out_specs=[pl.BlockSpec(memory_space=pltpu.VMEM)] * len(outs),
        compiler_params=pltpu.CompilerParams(vmem_limit_bytes=limit * 1024 * 1024),
        cost_estimate=cost(flops, sum(size(a) for a in ins) + sum(size(o) for o in outs), exps),
        name=name,
    )(*ins)


def like(shape, kind=BF16):
    return jax.ShapeDtypeStruct(shape, kind)


def scatter_chunk(own, other, core):
    ring = lax.axis_size("dp") // 2
    columns = own.shape[2]
    quarter = own.shape[1] // 2
    rows = quarter // ring
    low = (ring // 2) * rows
    (came,) = yield [(over("section"), other)]
    block = lambda t, x: pl.BlockSpec((1, quarter, columns), lambda i: (t, x, 0))
    whole = lambda size: pl.BlockSpec((size, columns), lambda i: (0, 0))

    def run(kernel, name, blocks, extra, outs):
        ins = [array for _ in blocks for array in (own, came)] + extra
        specs = [block(*spot) for spot in blocks for _ in (0, 1)]
        return pl.pallas_call(
            kernel,
            grid=(1,),
            out_shape=outs,
            in_specs=specs + [whole(array.shape[0]) for array in extra],
            out_specs=[whole(out.shape[0]) for out in outs],
            compiler_params=pltpu.CompilerParams(vmem_limit_bytes=14 * 1024 * 1024),
            cost_estimate=cost(0, 6 * quarter * columns * len(blocks)),
            name=name,
        )(*ins)

    first, second = run(
        partial(corner_kernel, low), "corner", [(1, 1)], [],
        [like((low, columns)), like((quarter - low, columns))],
    )
    first, second = yield [(over("tensor"), first), (pair_swap, second)]
    over_x, over_y = run(
        partial(sides_kernel, low), "sides", [(0, 1), (1, 0)], [first, second],
        [like((quarter, columns))] * 2,
    )
    over_x, over_y = yield [(pair_swap, over_x), (over("tensor"), over_y)]
    kinds = [F32] + [BF16] * (ring - 1)
    near = run(
        near_kernel, "near", [(0, 0)], [over_x, over_y], [like((rows, columns), k) for k in kinds]
    )
    total = yield from ring_scatter(near)
    to_core = lambda array: lax.ppermute(array, "section", [(1 - core, core)])
    (came,) = yield [(to_core, total.astype(BF16))]
    return total, came.astype(F32)


def attend_kernel(scale, q_ref, k0_ref, k1_ref, v0_ref, v1_ref, b0_ref, b1_ref, o_ref, lse_ref):
    span = q_ref.shape[0]
    lane = lax.broadcasted_iota(jnp.int32, (span, 128), 1)
    q = q_ref[...]
    k0, k1 = k0_ref[...], k1_ref[...]
    v0, v1 = v0_ref[...], v1_ref[...]
    b0, b1 = b0_ref[...], b1_ref[...]
    outs = []
    for head in (0, 1):
        own = (lane >= 64 * head) & (lane < 64 * head + 64)
        qh = jnp.where(own, q * jnp.asarray(scale, BF16), jnp.zeros_like(q))
        s0 = dot(k0, qh, COLS) + b0
        s1 = dot(k1, qh, COLS) + b1
        peak = jnp.maximum(jnp.max(s0, 0, keepdims=True), jnp.max(s1, 0, keepdims=True))
        p0 = jnp.exp(s0 - peak)
        p1 = jnp.exp(s1 - peak)
        total = jnp.sum(p0, 0, keepdims=True) + jnp.sum(p1, 0, keepdims=True)
        out = dot(v0, p0.astype(BF16), ROWS) + dot(v1, p1.astype(BF16), ROWS)
        outs.append(out / total)
        lse_ref[0, head : head + 1, :] = peak + jnp.log(total)
    row = lax.broadcasted_iota(jnp.int32, (128, span), 0)
    o_ref[...] = jnp.where(row < 64, outs[0], outs[1]).T.astype(BF16)


def attend(query, own, other, biases):
    _, span, width = query.shape
    groups = width // 128
    block = lambda first: pl.BlockSpec((None, span, 128), lambda t, g: (t, 0, first * groups + g))
    bias = pl.BlockSpec((span, 1), lambda t, g: (0, 0))
    return pl.pallas_call(
        partial(attend_kernel, 0.125),
        grid=(2, groups),
        out_shape=[like(query.shape), like((2, groups, 8, span), F32)],
        in_specs=[block(0), block(0), block(0), block(1), block(1), bias, bias],
        out_specs=[block(0), pl.BlockSpec((None, 1, 8, span), lambda t, g: (t, g, 0, 0))],
        compiler_params=pltpu.CompilerParams(vmem_limit_bytes=9 * 1024 * 1024),
        cost_estimate=cost(32 * groups * span * span * 2 * 128, 16 * span * width, 8 * groups * span * span),
        name="attend",
    )(query, own, other, own, other, *biases)


def attend_back_kernel(
    scale, q_ref, k0_ref, k1_ref, v0_ref, v1_ref, b0_ref, b1_ref, lse_ref, do_ref,
    near_ref, far_ref,
):
    span = q_ref.shape[0]
    lane = lax.broadcasted_iota(jnp.int32, (span, 128), 1)
    q, above = q_ref[...], do_ref[...]
    keys = (k0_ref[...], k1_ref[...])
    values = (v0_ref[...], v1_ref[...])
    biases = (b0_ref[...], b1_ref[...])
    dqs, dks, dvs = [], [], []
    for head in (0, 1):
        own = (lane >= 64 * head) & (lane < 64 * head + 64)
        qh = jnp.where(own, q * jnp.asarray(scale, BF16), jnp.zeros_like(q))
        ah = jnp.where(own, above, jnp.zeros_like(above))
        lse = lse_ref[0, head : head + 1, :]
        probs, pushed = [], []
        for part in (0, 1):
            probs.append(jnp.exp(dot(keys[part], qh, COLS) + biases[part] - lse))
            pushed.append(dot(values[part], ah, COLS))
        inner = jnp.sum(probs[0] * pushed[0], 0, keepdims=True) + jnp.sum(
            probs[1] * pushed[1], 0, keepdims=True
        )
        dq = None
        for part in (0, 1):
            slopes = (probs[part] * (pushed[part] - inner)).astype(BF16)
            piece = dot(keys[part], slopes, ROWS)
            dq = piece if dq is None else dq + piece
            dk = dot(slopes, qh)
            dv = dot(probs[part].astype(BF16), ah)
            if head == 0:
                dks.append(dk)
                dvs.append(dv)
            else:
                dks[part] = dks[part] + dk
                dvs[part] = dvs[part] + dv
        dqs.append(dq)
    row = lax.broadcasted_iota(jnp.int32, (128, span), 0)
    near_ref[0] = (jnp.where(row < 64, dqs[0], dqs[1]) * scale).T.astype(BF16)
    near_ref[1] = dks[0].astype(BF16)
    near_ref[2] = dvs[0].astype(BF16)
    far_ref[0] = dks[1].astype(BF16)
    far_ref[1] = dvs[1].astype(BF16)


def attend_back(query, own, other, biases, lse, above, t):
    _, span, width = query.shape
    groups = width // 128
    block = lambda first: pl.BlockSpec((None, span, 128), lambda g: (t, 0, first * groups + g))
    bias = pl.BlockSpec((span, 1), lambda g: (0, 0))
    return pl.pallas_call(
        partial(attend_back_kernel, 0.125),
        grid=(groups,),
        out_shape=[like((3, span, width)), like((2, span, width))],
        in_specs=[block(0), block(0), block(0), block(1), block(1), bias, bias]
        + [pl.BlockSpec((None, 1, 8, span), lambda g: (t, g, 0, 0)), block(0)],
        out_specs=[
            pl.BlockSpec((3, span, 128), lambda g: (0, 0, g)),
            pl.BlockSpec((2, span, 128), lambda g: (0, 0, g)),
        ],
        compiler_params=pltpu.CompilerParams(vmem_limit_bytes=14 * 1024 * 1024),
        cost_estimate=cost(40 * groups * span * span * 2 * 128, 12 * span * width, 4 * groups * span * span),
        name="attend_back",
    )(query, own, other, own, other, *biases, lse, above)


def normalised(values):
    centred = values - jnp.mean(values, -1, keepdims=True)
    scale = lax.rsqrt(jnp.mean(centred * centred, -1, keepdims=True) + 1e-05)
    return centred * scale, scale


def mixed_kernel(values, w0, w1, table, normed, query, own):
    third = query.shape[2]
    unit, _ = normalised(values[...])
    rows = (unit * (1.0 + table[0:1]) + table[1:2]).astype(BF16)
    normed[...] = rows
    for t, weight in enumerate((w0, w1)):
        cut = pl.ds(t * third, third)
        query[t] = (dot(rows, weight[:, :third]) + table[2:3, cut]).astype(BF16)
        own[t, :, :third] = dot(rows, weight[:, third : 2 * third]).astype(BF16)
        own[t, :, third:] = (dot(rows, weight[:, 2 * third : 3 * third]) + table[3:4, cut]).astype(BF16)


def mixed_forward(values, w_a, table):
    span, width = values.shape
    third = w_a[0].shape[1] // 4
    outs = [like((span, width)), like((2, span, third)), like((2, span, 2 * third))]
    return call(mixed_kernel, "mixed", [values, *w_a, table], outs, 2 * span * width * 6 * third)


def middle_kernel(values, attended, w0, w1, table, middle, normed):
    third = attended.shape[2]
    total = values[...] + table[4:5]
    for t, weight in enumerate((w0, w1)):
        total = total + dot(attended[t], weight[:, 3 * third :], COLS)
    middle[...] = total
    unit, _ = normalised(total)
    normed[...] = (unit * (1.0 + table[5:6]) + table[6:7]).astype(BF16)


def middle_forward(values, attended, w_a, table):
    span, width = values.shape
    outs = [like((span, width), F32), like((span, width))]
    return call(
        middle_kernel, "middle", [values, attended, *w_a, table], outs, 2 * span * width * width
    )


def hidden_kernel(normed, w0, w1, table, hidden, slope):
    width = table.shape[1]
    rows = normed[...]
    step = width // 2
    for t, weight in enumerate((w0, w1)):
        for start in range(0, hidden.shape[2], step):
            cut = slice(start, start + step)
            row = 8 + (t * hidden.shape[2] + start) // width
            column = (t * hidden.shape[2] + start) % width
            before = dot(rows, weight[:, cut]) + table[row : row + 1, column : column + step]
            share = 0.5 + 0.5 * lax.erf(before * (0.5**0.5))
            hidden[t, :, cut] = (before * share).astype(BF16)
            bell = jnp.exp(-0.5 * before * before) * 0.3989422804014327
            slope[t, :, cut] = (share + before * bell).astype(BF16)


def hidden_forward(normed, w_b, table):
    span, width = normed.shape
    unit = w_b[0].shape[1]
    outs = [like((2, span, unit))] * 2
    flops, exps = 4 * span * width * unit, 4 * span * unit
    return call(hidden_kernel, "hidden", [normed, *w_b, table], outs, flops, exps)


def down_kernel(middle, hidden, w0, w1, table, out):
    total = middle[...] + table[7:8]
    for t, weight in enumerate((w0, w1)):
        total = total + dot(hidden[t], weight[...], COLS)
    out[...] = total


def hidden_down(middle, hidden, w_c, table):
    span, width = middle.shape
    flops = 4 * span * width * w_c[0].shape[1]
    return call(down_kernel, "down", [middle, hidden, *w_c, table], [like((span, width), F32)], flops)[0]


def slope_kernel(short, w0, w1, slope, pushed):
    rows = short[...]
    step = rows.shape[1] // 2
    for t, weight in enumerate((w0, w1)):
        for start in range(0, slope.shape[2], step):
            cut = slice(start, start + step)
            grad = dot(rows, weight[:, cut]) * slope[t, :, cut].astype(F32)
            pushed[t, :, cut] = grad.astype(BF16)


def hidden_back(short, w_c, slope):
    flops = 2 * short.shape[1] * slope.size
    return call(slope_kernel, "hidden_back", [short, *w_c, slope], [like(slope.shape)], flops)[0]


def grads_kernel(count, *refs):
    outs = refs[-2:]
    start = 0
    for left, right in zip(refs[:count], refs[count : 2 * count]):
        half, size = left.shape[1] // 2, right.shape[2]
        for core, out in enumerate(outs):
            rows = left[:, core * half : (core + 1) * half].T
            for t in (0, 1):
                out[t, :, start : start + size] = dot(rows, right[t]).astype(BF16)
        start += size
    if len(refs) > 2 * count + 2:
        extra = refs[2 * count]
        half, size = extra.shape[0] // 2, extra.shape[1]
        for core, out in enumerate(outs):
            for t in (0, 1):
                out[t, :, start:] = extra[core * half : (core + 1) * half]


def grads_of(*pairs, extra=()):
    lefts, rights = [pair[0] for pair in pairs], [pair[1] for pair in pairs]
    half = lefts[0].shape[1] // 2
    total = sum(right.shape[2] for right in rights)
    flops = 8 * half * lefts[0].shape[0] * total
    total += sum(part.shape[1] for part in extra)
    outs = [like((2, half, total))] * 2
    ins = lefts + rights + list(extra)
    return call(partial(grads_kernel, len(pairs)), "grads", ins, outs, flops, limit=6)


def flat_kernel(near0, far0, near1, far1, flat):
    third = near0.shape[2]
    for t, (near, far) in enumerate(((near0, far0), (near1, far1))):
        for n in range(3):
            part = near[n]
            if n:
                part = (part.astype(F32) + far[n - 1].astype(F32)).astype(BF16)
            flat[t, :, n * third : (n + 1) * third] = part


def flat_of(near, far):
    _, span, third = near[0].shape
    ins = [near[0], far[0], near[1], far[1]]
    return call(flat_kernel, "flat", ins, [like((2, span, 3 * third))])[0]


def norm_back_kernel(gain, tail, add, parts, w0, w1, values, table, out, short, sums, columns, *above):
    size = parts.shape[2]
    weights = (w0, w1)
    grad = sum(dot(parts[t], weights[t][:, :size], COLS) for t in (0, 1))
    unit, scale = normalised(values[...])
    inner = grad * (1.0 + table[gain : gain + 1])
    inner = inner - jnp.mean(inner, -1, keepdims=True)
    inner = inner - unit * jnp.mean(inner * unit, -1, keepdims=True)
    total = add[...] + inner * scale
    out[...] = total
    low = total.astype(BF16)
    short[...] = low
    sums[0:1] = jnp.sum(grad * unit, 0, keepdims=True)
    sums[1:2] = jnp.sum(grad, 0, keepdims=True)
    sums[2:3] = jnp.sum(total, 0, keepdims=True)
    sums[3:4] = jnp.sum(add[...], 0, keepdims=True)
    for t in (0, 1):
        columns[t, 0:1] = jnp.sum(parts[t].astype(F32), 0, keepdims=True)


def norm_back(gain, add, parts, weights, values, table):
    span, width = values.shape
    size = parts.shape[2]
    outs = [
        like((span, width), F32), like((span, width)), like((8, width), F32), like((2, 8, size), F32),
    ]
    ins = [add, parts, *weights, values, table]
    return call(
        partial(norm_back_kernel, gain, 0), "norm_back", ins, outs, 4 * span * width * size
    )


def above_kernel(short, w0, w1, above):
    third = above.shape[2]
    for t, weight in enumerate((w0, w1)):
        above[t] = dot(short[...], weight[:, 3 * third :]).astype(BF16)


def attended_back(short, w_a):
    span, width = short.shape
    third = w_a[0].shape[1] // 4
    flops = 4 * span * width * third
    return call(above_kernel, "above", [short, *w_a], [like((2, span, third))], flops)[0]


def table_kernel(side, sums_in, columns_in, sums_mid, columns_mid, order, out):
    third = columns_in.shape[2] // 3
    width = order.shape[0]
    swapped = side[0] != 0

    def halves(parts):
        first = jnp.where(swapped, parts[1], parts[0])
        second = jnp.where(swapped, parts[0], parts[1])
        return [first, second]

    query = jnp.concatenate(halves([columns_in[t, 0:1, :third] for t in (0, 1)]), 1)
    value = jnp.concatenate(halves([columns_in[t, 0:1, 2 * third :] for t in (0, 1)]), 1)
    rise = halves([columns_mid[t, 0:1, :] for t in (0, 1)])
    rows = [query, value]
    for part in rise:
        rows += [part[:, :width], part[:, width:]]
    rows = jnp.concatenate(rows + [jnp.zeros((2, width), F32)], 0)
    rows = dot(rows.astype(BF16), order[...])
    table = [
        sums_in[0:2], rows[0:2], sums_mid[2:3], sums_mid[0:2], sums_mid[3:4], rows[2:6],
        jnp.zeros((out.shape[1] - 12, width), F32),
    ]
    out[...] = jnp.concatenate(table, 0).T.astype(BF16)


def table_back(side, sums_in, columns_in, sums_mid, columns_mid, order):
    ins = [side, sums_in, columns_in, sums_mid, columns_mid, order]
    specs = [pl.BlockSpec(memory_space=pltpu.SMEM)] + [pl.BlockSpec(memory_space=pltpu.VMEM)] * 5
    outs = [like((order.shape[0], 128))]
    return call(table_kernel, "table_back", ins, outs, specs=specs)[0]


def iter_swaps(rows, first, side, core):
    span, width = rows.shape
    to_core = lambda array: lax.ppermute(array, "section", [(1 - core, core)])
    (came,) = yield [(to_core, rows.astype(BF16))]
    came = came.astype(F32)
    full = jnp.stack([rows, came] if core == 0 else [came, rows])
    keep = lax.dynamic_index_in_dim(full, side, 0, keepdims=False)
    gone = lax.dynamic_index_in_dim(full, 1 - side, 0, keepdims=False).astype(BF16)
    pairs = [(2 * core, 2 * core + 1), (2 * core + 1, 2 * core)]
    (came,) = yield [(lambda array: lax.ppermute(array, ("section", "tensor"), pairs), gone)]
    came = came.astype(F32)
    return jnp.where(side == 0, jnp.stack([keep, came]), jnp.stack([came, keep]))


FEATURE_ROWS = (True, True, False, False, True, True, True, True, False, False, False, False)


def body(ends_in, lengths, vectors, w_qkv, w_out, w_up, w_down):
    core = lax.axis_index("section")
    first = core == 0
    side = lax.axis_index("tensor")
    count = lax.axis_size("dp")
    ring = count // 2
    rows = w_qkv.shape[1]
    half = rows // 2
    span, width = ends_in.shape[2:]
    third, unit = w_qkv.shape[-1], w_up.shape[-1]
    turned = side.astype(jnp.int32).reshape(1)

    at = jnp.arange(width, dtype=jnp.int32)
    row, rest = at % half, at // half
    step, rest = rest % ring, rest // ring
    spot = lax.axis_index("dp")
    owner = 2 * ((spot // 2 - step + ring) % ring) + (spot % 2 + rest % 2) % 2
    source = owner * rows + ((core + rest // 2) % 2) * half + row
    order = at[:, None] == source[None, :]
    order_low = order.astype(BF16)

    def to_own(array):
        return jnp.dot(array, order.astype(F32), precision=lax.Precision.HIGHEST)

    def from_own(array):
        return lax.dot_general(array, order.astype(F32), COLS, precision=lax.Precision.HIGHEST)

    index = spot * 2 + side
    cut = vectors.shape[-1]
    spread = lax.dynamic_update_slice_in_dim(
        jnp.zeros((vectors.shape[1], width), F32), vectors[0], index * cut, 1
    )
    own = jnp.concatenate([w_qkv[0].reshape(rows, -1), w_out[0].T, w_up[0], w_down[0].T], 1)
    halves = (own[:half], own[half:])
    came = swap(jnp.where(first, halves[1], halves[0]), "section")
    one, two = jnp.where(first, halves[0], came), jnp.where(first, came, halves[1])
    cuts = [slice(n * unit, (n + 1) * unit) for n in range(3)]
    chunks = [layer[:, c] for layer in (one,) for c in cuts]
    far_mine = lax.all_gather(two, ("dp", "tensor"), axis=0)
    a0 = Line(gather_chunk(chunks[0]))
    spread, ends = tied((spread, ends_in[0]), a0.sent)
    spread = spread + swap(spread, "tensor")
    spread, ends = lax.optimization_barrier((spread, ends))

    keep = lax.dynamic_index_in_dim(ends, side, 0, keepdims=False)
    gone = lax.dynamic_index_in_dim(ends, 1 - side, 0, keepdims=False)
    clip = swap(gone, "tensor")
    bit = 1
    while bit < count:
        spread = spread + pair_swap(spread, bit)
        bit *= 2
    theirs = swap(spread, "section")
    spread, theirs, clip, ready = join((spread, theirs, clip, chunks[1]), a0)
    b0 = Line(gather_chunk(ready))
    upper, lower = jnp.where(side == 0, keep, clip), jnp.where(side == 0, clip, keep)
    stay, leave = jnp.where(first, upper, lower), jnp.where(first, lower, upper)
    came = swap(leave, "section")
    values = dot(jnp.where(first, stay, came), order_low)
    upstream = dot(jnp.where(first, came, stay), order_low)
    up_short = upstream.astype(BF16)
    frames = lax.dynamic_index_in_dim(lengths, side, 0, keepdims=False)
    spots = lax.broadcasted_iota(jnp.int32, (span, 1), 0)
    biases = [
        jnp.where(spots + offset * span < frames, 0.0, -1e30).astype(F32)
        for offset in (core, 1 - core)
    ]
    is_feature = jnp.array(FEATURE_ROWS)[:, None]

    def sides_turned(table):
        heads = table[:8].reshape(8, 2, -1)
        rise = table[8:].reshape(2, 2, width)
        heads = jnp.where(side == 0, heads, heads[:, ::-1]).reshape(8, width)
        rise = jnp.where(side == 0, rise, rise[::-1]).reshape(4, width)
        return jnp.concatenate([heads, rise])

    def own_table(table):
        return jnp.where(is_feature, to_own(table), sides_turned(table))

    tables = [
        own_table(jnp.where(first, spread, theirs)),
        own_table(jnp.where(first, theirs, spread)),
    ]

    values, upstream, up_short, tables, ready = join(
        (values, upstream, up_short, tables, chunks[2]), a0, b0
    )
    c0 = Line(gather_chunk(ready))
    join((), a0)
    join((), a0)
    w_a0 = a0.result
    normed_0, query_0, own_0 = mixed_forward(values, w_a0, tables[0])
    other_0 = swap(own_0, "section")
    query_0, own_0, other_0 = join((query_0, own_0, other_0), b0)
    attended_0, logs_0 = attend(query_0, own_0, other_0, biases)
    attended_0 = join(attended_0, b0, c0)
    middle_0, short_0 = middle_forward(values, attended_0, w_a0, tables[0])
    short_0 = join(short_0, b0)
    w_b0 = b0.result
    hidden_0, slope_0 = hidden_forward(short_0, w_b0, tables[0])
    hidden_0, slope_0, far_mine = join((hidden_0, slope_0, far_mine), c0)
    far_theirs = swap(far_mine, "section")
    join((), c0)
    hidden_0 = join(hidden_0, c0)
    w_c0 = c0.result
    layer_one = hidden_down(middle_0, hidden_0, w_c0, tables[0])
    place = jnp.stack([spot // 2, spot % 2, side]).astype(jnp.int32)
    w_a1, w_b1, w_c1 = (pick(place, far_mine, far_theirs, n * unit, unit) for n in range(3))
    normed_1, query_1, own_1 = mixed_forward(layer_one, w_a1, tables[1])
    other_1 = swap(own_1, "section")
    attended_1, logs_1 = attend(query_1, own_1, other_1, biases)
    middle_1, short_1 = middle_forward(layer_one, attended_1, w_a1, tables[1])
    hidden_1, slope_1 = hidden_forward(short_1, w_b1, tables[1])
    grad_c = grads_of((up_short, hidden_1))
    sc1 = Line(scatter_chunk(*grad_c, 1))

    pushed_1 = hidden_back(up_short, w_c1, slope_1)
    pushed_1 = join(pushed_1, sc1)
    grad_mid_1, proj_1, sums_mid, columns_mid = norm_back(
        5, upstream, pushed_1, w_b1, middle_1, tables[1]
    )
    above_1 = attended_back(proj_1, w_a1)
    grad_bo = grads_of((short_1, pushed_1), (proj_1, attended_1))
    grad_bo, above_1 = join((grad_bo, above_1), sc1)
    sb1 = Line(scatter_chunk(*grad_bo, 1))
    near_a, far_a = attend_back(query_1, own_1, other_1, biases, logs_1, above_1, 0)
    near_a, far_a, above_1 = join((near_a, far_a, above_1), sb1, sc1)
    near_b, far_b = attend_back(query_1, own_1, other_1, biases, logs_1, above_1, 1)
    near_b, far_a, far_b = join((near_b, far_a, far_b), sb1)
    far_a, far_b = swap(far_a, "section"), swap(far_b, "section")
    flat_1 = flat_of((near_a, near_b), (far_a, far_b))
    grad_layer, back_short, sums_in, columns_in = norm_back(
        0, grad_mid_1, flat_1, w_a1, layer_one, tables[1]
    )
    table_1 = table_back(turned, sums_in, columns_in, sums_mid, columns_mid, order_low)
    grad_q = grads_of((normed_1, flat_1), extra=(table_1,))
    grad_q, back_short = join((grad_q, back_short), sb1, sc1)
    sq1 = Line(scatter_chunk(*grad_q, 1))
    grad_c = grads_of((back_short, hidden_0))
    pushed_0 = hidden_back(back_short, w_c0, slope_0)
    grad_c, pushed_0 = join((grad_c, pushed_0), sq1)
    sc0 = Line(scatter_chunk(*grad_c, 0))
    grad_mid_0, proj_0, sums_mid, columns_mid = norm_back(
        5, grad_layer, pushed_0, w_b0, middle_0, tables[0]
    )
    above_0 = attended_back(proj_0, w_a0)
    grad_bo = grads_of((short_0, pushed_0), (proj_0, attended_0))
    result = from_own(hidden_down(middle_1, hidden_1, w_c1, tables[1]))
    grad_bo, result, above_0 = join((grad_bo, result, above_0), sc0, sq1, sc1)
    out = Line(iter_swaps(result, first, side, 1))
    sb0 = Line(scatter_chunk(*grad_bo, 0))
    near_a, far_a = attend_back(query_0, own_0, other_0, biases, logs_0, above_0, 0)
    near_a, far_a, above_0 = join((near_a, far_a, above_0), sb0, sc0, sq1, sb1, out)
    near_b, far_b = attend_back(query_0, own_0, other_0, biases, logs_0, above_0, 1)
    near_b, far_a, far_b = join((near_b, far_a, far_b), sb0, sc0, sb1, sc1)
    far_a, far_b = swap(far_a, "section"), swap(far_b, "section")
    flat_0 = flat_of((near_a, near_b), (far_a, far_b))
    grad_values, _, sums_in, columns_in = norm_back(
        0, grad_mid_0, flat_0, w_a0, values, tables[0]
    )
    table_0 = table_back(turned, sums_in, columns_in, sums_mid, columns_mid, order_low)
    grad_q = grads_of((normed_0, flat_0), extra=(table_0,))
    grad_q = join(grad_q, sb0, sc0, sq1, out)
    sq0 = Line(scatter_chunk(*grad_q, 0))
    into = Line(iter_swaps(from_own(grad_values), first, side, 0), sq0.sent)
    join((), sq0, sc0, sq1)
    join((), sq0, into)
    join((), sq0, sb0)
    lines = [sq0, into, out, sb0, sc0, sq1, sb1, sc1]
    while any(not line.done for line in lines):
        join((), *lines)

    boundary = jnp.where(first, into.result, out.result)

    def cut_up(total, sizes):
        parts, start = [], 0
        for size in sizes:
            parts.append(total[:, start : start + size])
            start += size
        return parts

    three = 3 * third

    def sorted_parts(c, bo, qv):
        return (*cut_up(qv, (three, 128)), *cut_up(bo, (unit, third)), c)

    sums_0 = (sc0.result, sb0.result, sq0.result)
    sums_1 = (sc1.result, sb1.result, sq1.result)
    mine = [sorted_parts(*(total for total, _ in sums)) for sums in (sums_0, sums_1)]
    came = [sorted_parts(*(part for _, part in sums)) for sums in (sums_0, sums_1)]
    grads = [
        jnp.where(first, jnp.concatenate([g, g_far]), jnp.concatenate([h_far, h]))
        for g, g_far, h, h_far in zip(mine[0], came[0], mine[1], came[1])
    ]
    g_q, g_v, g_b, g_o, g_c = grads
    table_grad = lax.dynamic_slice_in_dim(g_v[:, :12], side * cut, cut, 0).T
    return (
        boundary[None],
        table_grad[None],
        g_q.reshape(w_qkv.shape),
        g_o.T[None],
        g_b[None],
        g_c.T[None],
    )


def solution(mesh):
    in_specs = (
        P("section", "dp", "tensor", None),
        P("dp"),
        P("section", None, ("dp", "tensor")),
        P("section", "dp", None, "tensor"),
        P("section", "tensor", "dp"),
        P("section", "dp", "tensor"),
        P("section", "tensor", "dp"),
    )
    out_specs = (
        P("section", "dp", "tensor", None),
        P("section", None, ("dp", "tensor")),
        P("section", "dp", None, "tensor"),
        P("section", "tensor", "dp"),
        P("section", "dp", "tensor"),
        P("section", "tensor", "dp"),
    )
    return jax.shard_map(body, mesh=mesh, in_specs=in_specs, out_specs=out_specs, check_vma=False)
```

```python
from functools import partial

import jax
import jax.numpy as jnp
from jax import lax
from jax.experimental import pallas as pl
from jax.experimental.pallas import tpu as pltpu
from jax.sharding import PartitionSpec as P

BF16 = jnp.bfloat16
F32 = jnp.float32
ROWS = (((0,), (0,)), ((), ()))
COLS = (((1,), (1,)), ((), ()))
PLAIN = (((1,), (0,)), ((), ()))
CROSS = ((0, 1), (1, 0))


def cost(flops, size, exps=0):
    return pl.CostEstimate(flops=flops, bytes_accessed=size, transcendentals=exps)


def dot(left, right, dims=PLAIN):
    return lax.dot_general(left, right, dims, preferred_element_type=F32)


def swap(array, axis):
    return lax.ppermute(array, axis, CROSS)


def pair_swap(array, bit=1):
    return lax.ppermute(array, "dp", [(i, i ^ bit) for i in range(lax.axis_size("dp"))])


def ring_shift(array, by):
    ring = lax.axis_size("dp") // 2
    pairs = [(2 * z + x, 2 * ((z + by) % ring) + x) for z in range(ring) for x in (0, 1)]
    return lax.ppermute(array, "dp", pairs)


def tied(state, after):
    return lax.optimization_barrier((state, after))[0] if after else state


class Line:
    def __init__(self, steps, after=()):
        self.steps, self.result, self.done = steps, None, False
        self.take(next(steps), after)

    def take(self, step, after):
        self.sent = tied([array for _, array in step], after)
        self.pending = [send(array) for (send, _), array in zip(step, self.sent)]

    def advance(self, arrays, after):
        try:
            self.take(self.steps.send(arrays), after)
        except StopIteration as end:
            self.result, self.done, self.pending, self.sent = end.value, True, [], []


def join(state, *lines):
    lines = [line for line in lines if not line.done]
    state, arrays = lax.optimization_barrier((state, [line.pending for line in lines]))
    sent = []
    for line, own in zip(lines, arrays):
        line.advance(own, sent)
        sent = sent + line.sent
    return tied(state, sent)


def over(axis):
    return lambda array: swap(array, axis)


def around(by):
    return lambda array: ring_shift(array, by)


def ring_gather(piece):
    ring = lax.axis_size("dp") // 2
    if ring <= 4:
        came = yield [(around(k), piece) for k in range(1, ring)]
        return [piece, *came]

    def step(k, state):
        moving, held = state
        moving = ring_shift(moving, 1)
        return moving, lax.dynamic_update_index_in_dim(held, moving, k, 0)

    held = jnp.zeros((ring,) + piece.shape, piece.dtype).at[0].set(piece)
    held = lax.fori_loop(1, ring, step, (piece, held))[1]
    return [held.reshape(-1, piece.shape[1])]


def ring_scatter(parts):
    ring = len(parts)
    if ring <= 4:
        came = yield [(around(-k), parts[k]) for k in range(1, ring)]
        return sum((part.astype(F32) for part in came), parts[0])

    stacked = jnp.stack([part.astype(BF16) for part in parts[1:]])

    def step(k, total):
        mine = lax.dynamic_index_in_dim(stacked, ring - 2 - k, 0, keepdims=False)
        return mine.astype(F32) + ring_shift(total.astype(BF16), -1).astype(F32)

    total = lax.fori_loop(1, ring - 1, step, stacked[ring - 2].astype(F32))
    return parts[0] + ring_shift(total.astype(BF16), -1).astype(F32)


def copy_kernel(plan, count, *refs):
    sources, outs, sems = refs[:count], refs[count:-1], refs[-1]
    copies = []
    for source, (out, row) in zip(sources, plan):
        copies.append(
            pltpu.make_async_copy(
                source, outs[out].at[pl.ds(row, source.shape[0])], sems.at[len(copies)]
            )
        )
    for copy in copies:
        copy.start()
    for copy in copies:
        copy.wait()


def stack_rows(*groups):
    sources = [part for group in groups for part in group]
    plan, outs = [], []
    for index, group in enumerate(groups):
        row = 0
        for part in group:
            plan.append((index, row))
            row += part.shape[0]
        outs.append(jax.ShapeDtypeStruct((row,) + group[0].shape[1:], group[0].dtype))
    return pl.pallas_call(
        partial(copy_kernel, plan, len(sources)),
        out_shape=outs,
        in_specs=[pl.BlockSpec(memory_space=pl.ANY)] * len(sources),
        out_specs=[pl.BlockSpec(memory_space=pltpu.VMEM)] * len(outs),
        scratch_shapes=[pltpu.SemaphoreType.DMA((len(sources),))],
        compiler_params=pltpu.CompilerParams(vmem_limit_bytes=(1 << 20) + sum(2 * out.size for out in outs)),
        cost_estimate=cost(0, sum(4 * part.size for part in sources)),
        name="stack_rows",
    )(*sources)


def gather_chunk(piece):
    rows, columns = piece.shape
    low = (lax.axis_size("dp") // 4) * rows
    near = yield from ring_gather(piece)
    near = stack_rows(near)[0] if len(near) > 1 and rows % 16 == 0 else jnp.concatenate(near)
    over_x, over_y = yield [(pair_swap, near), (over("tensor"), near)]
    first, second = yield [(over("tensor"), over_x[:low]), (pair_swap, over_y[low:])]
    mine = stack_rows([near, over_x, over_y, first, second])[0]
    mine = mine.reshape(2, -1, columns)
    (theirs,) = yield [(over("section"), mine)]
    return stack_rows([mine[0], theirs[0]], [mine[1], theirs[1]])


def pick_kernel(ring, column, place, mine, theirs, out0, out1, sems):
    z, x, y = place[0], place[1], place[2]
    rows, columns = mine.shape[1], out0.shape[1]
    copies = []
    for ds, source in enumerate((mine, theirs)):
        for dx in (0, 1):
            for k in range(ring):
                owner = 2 * lax.rem(z - k + ring, ring) + (x + dx) % 2
                row = ((ds * 2 + dx) * ring + k) * rows
                for dy, out in enumerate((out0, out1)):
                    copies.append(
                        pltpu.make_async_copy(
                            source.at[2 * owner + (y + dy) % 2, :, pl.ds(column, columns)],
                            out.at[pl.ds(row, rows)],
                            sems.at[len(copies)],
                        )
                    )
    for copy in copies:
        copy.start()
    for copy in copies:
        copy.wait()


def pick(place, mine, theirs, column, columns):
    groups, rows, _ = mine.shape
    ring = groups // 4
    if rows % 16:
        return pick_plain(place, mine, theirs, column, columns)
    out = like((groups * rows, columns))
    return pl.pallas_call(
        partial(pick_kernel, ring, column),
        out_shape=[out, out],
        in_specs=[pl.BlockSpec(memory_space=pltpu.SMEM)] + [pl.BlockSpec(memory_space=pl.ANY)] * 2,
        out_specs=[pl.BlockSpec(memory_space=pltpu.VMEM)] * 2,
        scratch_shapes=[pltpu.SemaphoreType.DMA((2 * groups,))],
        compiler_params=pltpu.CompilerParams(vmem_limit_bytes=6 * 1024 * 1024),
        cost_estimate=cost(0, 4 * groups * rows * columns),
        name="pick",
    )(place, mine, theirs)


def pick_plain(place, mine, theirs, column, columns):
    groups, rows, _ = mine.shape
    ring = groups // 4
    near = jnp.arange(groups // 2) % ring
    owner = 2 * ((place[0] - near + ring) % ring) + (place[1] + jnp.arange(groups // 2) // ring) % 2
    outs = []
    for dy in (0, 1):
        which = 2 * owner + (place[2] + dy) % 2
        parts = [part[:, :, column : column + columns][which] for part in (mine, theirs)]
        outs.append(jnp.concatenate(parts).reshape(-1, columns))
    return outs


def total_of(own, came):
    return own[0].astype(F32) + came[0].astype(F32)


def corner_kernel(low, own, came, first, second):
    total = total_of(own, came)
    first[...] = total[:low].astype(BF16)
    second[...] = total[low:].astype(BF16)


def sides_kernel(low, own_x, came_x, own_y, came_y, first, second, over_x, over_y):
    total = total_of(own_x, came_x)
    over_x[:low] = (total[:low] + first[...].astype(F32)).astype(BF16)
    over_x[low:] = total[low:].astype(BF16)
    total = total_of(own_y, came_y)
    over_y[:low] = total[:low].astype(BF16)
    over_y[low:] = (total[low:] + second[...].astype(F32)).astype(BF16)


def near_kernel(own, came, over_x, over_y, *near):
    total = total_of(own, came) + over_x[...].astype(F32) + over_y[...].astype(F32)
    rows = near[0].shape[0]
    for k, out in enumerate(near):
        out[...] = total[k * rows : (k + 1) * rows].astype(out.dtype)


def call(kernel, name, ins, outs, flops=0, exps=0, limit=5, specs=None, aliases=None):
    size = lambda a: a.size * a.dtype.itemsize
    return pl.pallas_call(
        kernel,
        out_shape=outs,
        in_specs=specs or [pl.BlockSpec(memory_space=pltpu.VMEM)] * len(ins),
        out_specs=[pl.BlockSpec(memory_space=pltpu.VMEM)] * len(outs),
        compiler_params=pltpu.CompilerParams(vmem_limit_bytes=limit * 1024 * 1024),
        cost_estimate=cost(flops, sum(size(a) for a in ins) + sum(size(o) for o in outs), exps),
        name=name,
    )(*ins)


def like(shape, kind=BF16):
    return jax.ShapeDtypeStruct(shape, kind)


def scatter_chunk(own, other, core):
    ring = lax.axis_size("dp") // 2
    columns = own.shape[2]
    quarter = own.shape[1] // 2
    rows = quarter // ring
    low = (ring // 2) * rows
    (came,) = yield [(over("section"), other)]
    block = lambda t, x: pl.BlockSpec((1, quarter, columns), lambda i: (t, x, 0))
    whole = lambda size: pl.BlockSpec((size, columns), lambda i: (0, 0))

    def run(kernel, name, blocks, extra, outs):
        ins = [array for _ in blocks for array in (own, came)] + extra
        specs = [block(*spot) for spot in blocks for _ in (0, 1)]
        return pl.pallas_call(
            kernel,
            grid=(1,),
            out_shape=outs,
            in_specs=specs + [whole(array.shape[0]) for array in extra],
            out_specs=[whole(out.shape[0]) for out in outs],
            compiler_params=pltpu.CompilerParams(vmem_limit_bytes=14 * 1024 * 1024),
            cost_estimate=cost(0, 6 * quarter * columns * len(blocks)),
            name=name,
        )(*ins)

    first, second = run(
        partial(corner_kernel, low), "corner", [(1, 1)], [],
        [like((low, columns)), like((quarter - low, columns))],
    )
    first, second = yield [(over("tensor"), first), (pair_swap, second)]
    over_x, over_y = run(
        partial(sides_kernel, low), "sides", [(0, 1), (1, 0)], [first, second],
        [like((quarter, columns))] * 2,
    )
    over_x, over_y = yield [(pair_swap, over_x), (over("tensor"), over_y)]
    kinds = [F32] + [BF16] * (ring - 1)
    near = run(
        near_kernel, "near", [(0, 0)], [over_x, over_y], [like((rows, columns), k) for k in kinds]
    )
    total = yield from ring_scatter(near)
    to_core = lambda array: lax.ppermute(array, "section", [(1 - core, core)])
    (came,) = yield [(to_core, total.astype(BF16))]
    return total, came.astype(F32)


def attend_kernel(scale, q_ref, k0_ref, k1_ref, v0_ref, v1_ref, b0_ref, b1_ref, o_ref, lse_ref):
    span = q_ref.shape[0]
    lane = lax.broadcasted_iota(jnp.int32, (span, 128), 1)
    q = q_ref[...]
    k0, k1 = k0_ref[...], k1_ref[...]
    v0, v1 = v0_ref[...], v1_ref[...]
    b0, b1 = b0_ref[...], b1_ref[...]
    outs = []
    for head in (0, 1):
        own = (lane >= 64 * head) & (lane < 64 * head + 64)
        qh = jnp.where(own, q * jnp.asarray(scale, BF16), jnp.zeros_like(q))
        s0 = dot(k0, qh, COLS) + b0
        s1 = dot(k1, qh, COLS) + b1
        peak = jnp.maximum(jnp.max(s0, 0, keepdims=True), jnp.max(s1, 0, keepdims=True))
        p0 = jnp.exp(s0 - peak)
        p1 = jnp.exp(s1 - peak)
        total = jnp.sum(p0, 0, keepdims=True) + jnp.sum(p1, 0, keepdims=True)
        out = dot(v0, p0.astype(BF16), ROWS) + dot(v1, p1.astype(BF16), ROWS)
        outs.append(out / total)
        lse_ref[0, head : head + 1, :] = peak + jnp.log(total)
    row = lax.broadcasted_iota(jnp.int32, (128, span), 0)
    o_ref[...] = jnp.where(row < 64, outs[0], outs[1]).T.astype(BF16)


def attend(query, own, other, biases):
    _, span, width = query.shape
    groups = width // 128
    block = lambda first: pl.BlockSpec((None, span, 128), lambda t, g: (t, 0, first * groups + g))
    bias = pl.BlockSpec((span, 1), lambda t, g: (0, 0))
    return pl.pallas_call(
        partial(attend_kernel, 0.125),
        grid=(2, groups),
        out_shape=[like(query.shape), like((2, groups, 8, span), F32)],
        in_specs=[block(0), block(0), block(0), block(1), block(1), bias, bias],
        out_specs=[block(0), pl.BlockSpec((None, 1, 8, span), lambda t, g: (t, g, 0, 0))],
        compiler_params=pltpu.CompilerParams(vmem_limit_bytes=9 * 1024 * 1024),
        cost_estimate=cost(32 * groups * span * span * 2 * 128, 16 * span * width, 8 * groups * span * span),
        name="attend",
    )(query, own, other, own, other, *biases)


def attend_back_kernel(
    scale, q_ref, k0_ref, k1_ref, v0_ref, v1_ref, b0_ref, b1_ref, lse_ref, do_ref,
    near_ref, far_ref,
):
    span = q_ref.shape[0]
    lane = lax.broadcasted_iota(jnp.int32, (span, 128), 1)
    q, above = q_ref[...], do_ref[...]
    keys = (k0_ref[...], k1_ref[...])
    values = (v0_ref[...], v1_ref[...])
    biases = (b0_ref[...], b1_ref[...])
    dqs, dks, dvs = [], [], []
    for head in (0, 1):
        own = (lane >= 64 * head) & (lane < 64 * head + 64)
        qh = jnp.where(own, q * jnp.asarray(scale, BF16), jnp.zeros_like(q))
        ah = jnp.where(own, above, jnp.zeros_like(above))
        lse = lse_ref[0, head : head + 1, :]
        probs, pushed = [], []
        for part in (0, 1):
            probs.append(jnp.exp(dot(keys[part], qh, COLS) + biases[part] - lse))
            pushed.append(dot(values[part], ah, COLS))
        inner = jnp.sum(probs[0] * pushed[0], 0, keepdims=True) + jnp.sum(
            probs[1] * pushed[1], 0, keepdims=True
        )
        dq = None
        for part in (0, 1):
            slopes = (probs[part] * (pushed[part] - inner)).astype(BF16)
            piece = dot(keys[part], slopes, ROWS)
            dq = piece if dq is None else dq + piece
            dk = dot(slopes, qh)
            dv = dot(probs[part].astype(BF16), ah)
            if head == 0:
                dks.append(dk)
                dvs.append(dv)
            else:
                dks[part] = dks[part] + dk
                dvs[part] = dvs[part] + dv
        dqs.append(dq)
    row = lax.broadcasted_iota(jnp.int32, (128, span), 0)
    near_ref[0] = (jnp.where(row < 64, dqs[0], dqs[1]) * scale).T.astype(BF16)
    near_ref[1] = dks[0].astype(BF16)
    near_ref[2] = dvs[0].astype(BF16)
    far_ref[0] = dks[1].astype(BF16)
    far_ref[1] = dvs[1].astype(BF16)


def attend_back(query, own, other, biases, lse, above, t):
    _, span, width = query.shape
    groups = width // 128
    block = lambda first: pl.BlockSpec((None, span, 128), lambda g: (t, 0, first * groups + g))
    bias = pl.BlockSpec((span, 1), lambda g: (0, 0))
    return pl.pallas_call(
        partial(attend_back_kernel, 0.125),
        grid=(groups,),
        out_shape=[like((3, span, width)), like((2, span, width))],
        in_specs=[block(0), block(0), block(0), block(1), block(1), bias, bias]
        + [pl.BlockSpec((None, 1, 8, span), lambda g: (t, g, 0, 0)), block(0)],
        out_specs=[
            pl.BlockSpec((3, span, 128), lambda g: (0, 0, g)),
            pl.BlockSpec((2, span, 128), lambda g: (0, 0, g)),
        ],
        compiler_params=pltpu.CompilerParams(vmem_limit_bytes=14 * 1024 * 1024),
        cost_estimate=cost(40 * groups * span * span * 2 * 128, 12 * span * width, 4 * groups * span * span),
        name="attend_back",
    )(query, own, other, own, other, *biases, lse, above)


def normalised(values):
    centred = values - jnp.mean(values, -1, keepdims=True)
    scale = lax.rsqrt(jnp.mean(centred * centred, -1, keepdims=True) + 1e-05)
    return centred * scale, scale


def mixed_kernel(values, w0, w1, table, normed, query, own):
    third = query.shape[2]
    unit, _ = normalised(values[...])
    rows = (unit * (1.0 + table[0:1]) + table[1:2]).astype(BF16)
    normed[...] = rows
    for t, weight in enumerate((w0, w1)):
        cut = pl.ds(t * third, third)
        query[t] = (dot(rows, weight[:, :third]) + table[2:3, cut]).astype(BF16)
        own[t, :, :third] = dot(rows, weight[:, third : 2 * third]).astype(BF16)
        own[t, :, third:] = (dot(rows, weight[:, 2 * third : 3 * third]) + table[3:4, cut]).astype(BF16)


def mixed_forward(values, w_a, table):
    span, width = values.shape
    third = w_a[0].shape[1] // 4
    outs = [like((span, width)), like((2, span, third)), like((2, span, 2 * third))]
    return call(mixed_kernel, "mixed", [values, *w_a, table], outs, 2 * span * width * 6 * third)


def middle_kernel(values, attended, w0, w1, table, middle, normed):
    third = attended.shape[2]
    total = values[...] + table[4:5]
    for t, weight in enumerate((w0, w1)):
        total = total + dot(attended[t], weight[:, 3 * third :], COLS)
    middle[...] = total
    unit, _ = normalised(total)
    normed[...] = (unit * (1.0 + table[5:6]) + table[6:7]).astype(BF16)


def middle_forward(values, attended, w_a, table):
    span, width = values.shape
    outs = [like((span, width), F32), like((span, width))]
    return call(
        middle_kernel, "middle", [values, attended, *w_a, table], outs, 2 * span * width * width
    )


def hidden_kernel(normed, w0, w1, table, hidden, slope):
    width = table.shape[1]
    rows = normed[...]
    step = width // 2
    for t, weight in enumerate((w0, w1)):
        for start in range(0, hidden.shape[2], step):
            cut = slice(start, start + step)
            row = 8 + (t * hidden.shape[2] + start) // width
            column = (t * hidden.shape[2] + start) % width
            before = dot(rows, weight[:, cut]) + table[row : row + 1, column : column + step]
            share = 0.5 + 0.5 * lax.erf(before * (0.5**0.5))
            hidden[t, :, cut] = (before * share).astype(BF16)
            bell = jnp.exp(-0.5 * before * before) * 0.3989422804014327
            slope[t, :, cut] = (share + before * bell).astype(BF16)


def hidden_forward(normed, w_b, table):
    span, width = normed.shape
    unit = w_b[0].shape[1]
    outs = [like((2, span, unit))] * 2
    flops, exps = 4 * span * width * unit, 4 * span * unit
    return call(hidden_kernel, "hidden", [normed, *w_b, table], outs, flops, exps)


def down_kernel(middle, hidden, w0, w1, table, out):
    total = middle[...] + table[7:8]
    for t, weight in enumerate((w0, w1)):
        total = total + dot(hidden[t], weight[...], COLS)
    out[...] = total


def hidden_down(middle, hidden, w_c, table):
    span, width = middle.shape
    flops = 4 * span * width * w_c[0].shape[1]
    return call(down_kernel, "down", [middle, hidden, *w_c, table], [like((span, width), F32)], flops)[0]


def slope_kernel(short, w0, w1, slope, pushed):
    rows = short[...]
    step = rows.shape[1] // 2
    for t, weight in enumerate((w0, w1)):
        for start in range(0, slope.shape[2], step):
            cut = slice(start, start + step)
            grad = dot(rows, weight[:, cut]) * slope[t, :, cut].astype(F32)
            pushed[t, :, cut] = grad.astype(BF16)


def hidden_back(short, w_c, slope):
    flops = 2 * short.shape[1] * slope.size
    return call(slope_kernel, "hidden_back", [short, *w_c, slope], [like(slope.shape)], flops)[0]


def grads_kernel(count, *refs):
    outs = refs[-2:]
    start = 0
    for left, right in zip(refs[:count], refs[count : 2 * count]):
        half, size = left.shape[1] // 2, right.shape[2]
        for core, out in enumerate(outs):
            rows = left[:, core * half : (core + 1) * half].T
            for t in (0, 1):
                out[t, :, start : start + size] = dot(rows, right[t]).astype(BF16)
        start += size
    if len(refs) > 2 * count + 2:
        extra = refs[2 * count]
        half, size = extra.shape[0] // 2, extra.shape[1]
        for core, out in enumerate(outs):
            for t in (0, 1):
                out[t, :, start:] = extra[core * half : (core + 1) * half]


def grads_of(*pairs, extra=()):
    lefts, rights = [pair[0] for pair in pairs], [pair[1] for pair in pairs]
    half = lefts[0].shape[1] // 2
    total = sum(right.shape[2] for right in rights)
    flops = 8 * half * lefts[0].shape[0] * total
    total += sum(part.shape[1] for part in extra)
    outs = [like((2, half, total))] * 2
    ins = lefts + rights + list(extra)
    return call(partial(grads_kernel, len(pairs)), "grads", ins, outs, flops, limit=6)


def flat_kernel(near0, far0, near1, far1, flat):
    third = near0.shape[2]
    for t, (near, far) in enumerate(((near0, far0), (near1, far1))):
        for n in range(3):
            part = near[n]
            if n:
                part = (part.astype(F32) + far[n - 1].astype(F32)).astype(BF16)
            flat[t, :, n * third : (n + 1) * third] = part


def flat_of(near, far):
    _, span, third = near[0].shape
    ins = [near[0], far[0], near[1], far[1]]
    return call(flat_kernel, "flat", ins, [like((2, span, 3 * third))])[0]


def norm_back_kernel(gain, tail, add, parts, w0, w1, values, table, out, short, sums, columns, *above):
    size = parts.shape[2]
    weights = (w0, w1)
    grad = sum(dot(parts[t], weights[t][:, :size], COLS) for t in (0, 1))
    unit, scale = normalised(values[...])
    inner = grad * (1.0 + table[gain : gain + 1])
    inner = inner - jnp.mean(inner, -1, keepdims=True)
    inner = inner - unit * jnp.mean(inner * unit, -1, keepdims=True)
    total = add[...] + inner * scale
    out[...] = total
    low = total.astype(BF16)
    short[...] = low
    sums[0:1] = jnp.sum(grad * unit, 0, keepdims=True)
    sums[1:2] = jnp.sum(grad, 0, keepdims=True)
    sums[2:3] = jnp.sum(total, 0, keepdims=True)
    sums[3:4] = jnp.sum(add[...], 0, keepdims=True)
    for t in (0, 1):
        columns[t, 0:1] = jnp.sum(parts[t].astype(F32), 0, keepdims=True)


def norm_back(gain, add, parts, weights, values, table):
    span, width = values.shape
    size = parts.shape[2]
    outs = [
        like((span, width), F32), like((span, width)), like((8, width), F32), like((2, 8, size), F32),
    ]
    ins = [add, parts, *weights, values, table]
    return call(
        partial(norm_back_kernel, gain, 0), "norm_back", ins, outs, 4 * span * width * size
    )


def above_kernel(short, w0, w1, above):
    third = above.shape[2]
    for t, weight in enumerate((w0, w1)):
        above[t] = dot(short[...], weight[:, 3 * third :]).astype(BF16)


def attended_back(short, w_a):
    span, width = short.shape
    third = w_a[0].shape[1] // 4
    flops = 4 * span * width * third
    return call(above_kernel, "above", [short, *w_a], [like((2, span, third))], flops)[0]


def table_kernel(side, sums_in, columns_in, sums_mid, columns_mid, order, out):
    third = columns_in.shape[2] // 3
    width = order.shape[0]
    swapped = side[0] != 0

    def halves(parts):
        first = jnp.where(swapped, parts[1], parts[0])
        second = jnp.where(swapped, parts[0], parts[1])
        return [first, second]

    query = jnp.concatenate(halves([columns_in[t, 0:1, :third] for t in (0, 1)]), 1)
    value = jnp.concatenate(halves([columns_in[t, 0:1, 2 * third :] for t in (0, 1)]), 1)
    rise = halves([columns_mid[t, 0:1, :] for t in (0, 1)])
    rows = [query, value]
    for part in rise:
        rows += [part[:, :width], part[:, width:]]
    rows = jnp.concatenate(rows + [jnp.zeros((2, width), F32)], 0)
    rows = dot(rows.astype(BF16), order[...])
    table = [
        sums_in[0:2], rows[0:2], sums_mid[2:3], sums_mid[0:2], sums_mid[3:4], rows[2:6],
        jnp.zeros((out.shape[1] - 12, width), F32),
    ]
    out[...] = jnp.concatenate(table, 0).T.astype(BF16)


def table_back(side, sums_in, columns_in, sums_mid, columns_mid, order):
    ins = [side, sums_in, columns_in, sums_mid, columns_mid, order]
    specs = [pl.BlockSpec(memory_space=pltpu.SMEM)] + [pl.BlockSpec(memory_space=pltpu.VMEM)] * 5
    outs = [like((order.shape[0], 128))]
    return call(table_kernel, "table_back", ins, outs, specs=specs)[0]


def iter_swaps(rows, first, side, core):
    span, width = rows.shape
    to_core = lambda array: lax.ppermute(array, "section", [(1 - core, core)])
    (came,) = yield [(to_core, rows.astype(BF16))]
    came = came.astype(F32)
    full = jnp.stack([rows, came] if core == 0 else [came, rows])
    keep = lax.dynamic_index_in_dim(full, side, 0, keepdims=False)
    gone = lax.dynamic_index_in_dim(full, 1 - side, 0, keepdims=False).astype(BF16)
    pairs = [(2 * core, 2 * core + 1), (2 * core + 1, 2 * core)]
    (came,) = yield [(lambda array: lax.ppermute(array, ("section", "tensor"), pairs), gone)]
    came = came.astype(F32)
    return jnp.where(side == 0, jnp.stack([keep, came]), jnp.stack([came, keep]))


FEATURE_ROWS = (True, True, False, False, True, True, True, True, False, False, False, False)


def body(ends_in, lengths, vectors, w_qkv, w_out, w_up, w_down):
    core = lax.axis_index("section")
    first = core == 0
    side = lax.axis_index("tensor")
    count = lax.axis_size("dp")
    ring = count // 2
    rows = w_qkv.shape[1]
    half = rows // 2
    span, width = ends_in.shape[2:]
    third, unit = w_qkv.shape[-1], w_up.shape[-1]
    turned = side.astype(jnp.int32).reshape(1)

    at = jnp.arange(width, dtype=jnp.int32)
    row, rest = at % half, at // half
    step, rest = rest % ring, rest // ring
    spot = lax.axis_index("dp")
    owner = 2 * ((spot // 2 - step + ring) % ring) + (spot % 2 + rest % 2) % 2
    source = owner * rows + ((core + rest // 2) % 2) * half + row
    order = at[:, None] == source[None, :]
    order_low = order.astype(BF16)

    def to_own(array):
        return jnp.dot(array, order.astype(F32), precision=lax.Precision.HIGHEST)

    def from_own(array):
        return lax.dot_general(array, order.astype(F32), COLS, precision=lax.Precision.HIGHEST)

    index = spot * 2 + side
    cut = vectors.shape[-1]
    spread = lax.dynamic_update_slice_in_dim(
        jnp.zeros((vectors.shape[1], width), F32), vectors[0], index * cut, 1
    )
    own = jnp.concatenate([w_qkv[0].reshape(rows, -1), w_out[0].T, w_up[0], w_down[0].T], 1)
    halves = (own[:half], own[half:])
    came = swap(jnp.where(first, halves[1], halves[0]), "section")
    one, two = jnp.where(first, halves[0], came), jnp.where(first, came, halves[1])
    cuts = [slice(n * unit, (n + 1) * unit) for n in range(3)]
    chunks = [layer[:, c] for layer in (one,) for c in cuts]
    far_mine = lax.all_gather(two[:, : 2 * unit], ("dp", "tensor"), axis=0)
    a0 = Line(gather_chunk(chunks[0]))
    spread, ends = tied((spread, ends_in[0]), a0.sent)
    spread = spread + swap(spread, "tensor")
    spread, ends = lax.optimization_barrier((spread, ends))

    keep = lax.dynamic_index_in_dim(ends, side, 0, keepdims=False)
    gone = lax.dynamic_index_in_dim(ends, 1 - side, 0, keepdims=False)
    clip = swap(gone, "tensor")
    bit = 1
    while bit < count:
        spread = spread + pair_swap(spread, bit)
        bit *= 2
    theirs = swap(spread, "section")
    spread, theirs, clip, ready = join((spread, theirs, clip, chunks[1]), a0)
    b0 = Line(gather_chunk(ready))
    upper, lower = jnp.where(side == 0, keep, clip), jnp.where(side == 0, clip, keep)
    stay, leave = jnp.where(first, upper, lower), jnp.where(first, lower, upper)
    came = swap(leave, "section")
    values = dot(jnp.where(first, stay, came), order_low)
    upstream = dot(jnp.where(first, came, stay), order_low)
    up_short = upstream.astype(BF16)
    frames = lax.dynamic_index_in_dim(lengths, side, 0, keepdims=False)
    spots = lax.broadcasted_iota(jnp.int32, (span, 1), 0)
    biases = [
        jnp.where(spots + offset * span < frames, 0.0, -1e30).astype(F32)
        for offset in (core, 1 - core)
    ]
    is_feature = jnp.array(FEATURE_ROWS)[:, None]

    def sides_turned(table):
        heads = table[:8].reshape(8, 2, -1)
        rise = table[8:].reshape(2, 2, width)
        heads = jnp.where(side == 0, heads, heads[:, ::-1]).reshape(8, width)
        rise = jnp.where(side == 0, rise, rise[::-1]).reshape(4, width)
        return jnp.concatenate([heads, rise])

    def own_table(table):
        return jnp.where(is_feature, to_own(table), sides_turned(table))

    tables = [
        own_table(jnp.where(first, spread, theirs)),
        own_table(jnp.where(first, theirs, spread)),
    ]

    values, upstream, up_short, tables, ready = join(
        (values, upstream, up_short, tables, chunks[2]), a0, b0
    )
    c0 = Line(gather_chunk(ready))
    join((), a0)
    join((), a0)
    w_a0 = a0.result
    normed_0, query_0, own_0 = mixed_forward(values, w_a0, tables[0])
    other_0 = swap(own_0, "section")
    query_0, own_0, other_0 = join((query_0, own_0, other_0), b0)
    attended_0, logs_0 = attend(query_0, own_0, other_0, biases)
    attended_0 = join(attended_0, b0, c0)
    middle_0, short_0 = middle_forward(values, attended_0, w_a0, tables[0])
    short_0 = join(short_0, b0)
    w_b0 = b0.result
    hidden_0, slope_0 = hidden_forward(short_0, w_b0, tables[0])
    hidden_0, slope_0, far_mine, ready = join((hidden_0, slope_0, far_mine, two[:, 2 * unit :]), c0)
    far_theirs = swap(far_mine, "section")
    c1 = Line(gather_chunk(ready))
    join((), c0)
    hidden_0 = join(hidden_0, c0)
    w_c0 = c0.result
    layer_one = hidden_down(middle_0, hidden_0, w_c0, tables[0])
    place = jnp.stack([spot // 2, spot % 2, side]).astype(jnp.int32)
    layer_one = join(layer_one, c1)
    w_a1, w_b1 = (pick(place, far_mine, far_theirs, n * unit, unit) for n in (0, 1))
    normed_1, query_1, own_1 = mixed_forward(layer_one, w_a1, tables[1])
    other_1 = swap(own_1, "section")
    attended_1, logs_1 = attend(query_1, own_1, other_1, biases)
    attended_1 = join(attended_1, c1)
    middle_1, short_1 = middle_forward(layer_one, attended_1, w_a1, tables[1])
    hidden_1, slope_1 = hidden_forward(short_1, w_b1, tables[1])
    hidden_1, slope_1 = join((hidden_1, slope_1), c1)
    grad_c = grads_of((up_short, hidden_1))
    grad_c = join(grad_c, c1)
    w_c1 = c1.result
    sc1 = Line(scatter_chunk(*grad_c, 1))

    pushed_1 = hidden_back(up_short, w_c1, slope_1)
    pushed_1 = join(pushed_1, sc1)
    grad_mid_1, proj_1, sums_mid, columns_mid = norm_back(
        5, upstream, pushed_1, w_b1, middle_1, tables[1]
    )
    above_1 = attended_back(proj_1, w_a1)
    grad_bo = grads_of((short_1, pushed_1), (proj_1, attended_1))
    grad_bo, above_1 = join((grad_bo, above_1), sc1)
    sb1 = Line(scatter_chunk(*grad_bo, 1))
    near_a, far_a = attend_back(query_1, own_1, other_1, biases, logs_1, above_1, 0)
    near_a, far_a, above_1 = join((near_a, far_a, above_1), sb1, sc1)
    near_b, far_b = attend_back(query_1, own_1, other_1, biases, logs_1, above_1, 1)
    near_b, far_a, far_b = join((near_b, far_a, far_b), sb1)
    far_a, far_b = swap(far_a, "section"), swap(far_b, "section")
    flat_1 = flat_of((near_a, near_b), (far_a, far_b))
    grad_layer, back_short, sums_in, columns_in = norm_back(
        0, grad_mid_1, flat_1, w_a1, layer_one, tables[1]
    )
    table_1 = table_back(turned, sums_in, columns_in, sums_mid, columns_mid, order_low)
    grad_q = grads_of((normed_1, flat_1), extra=(table_1,))
    grad_q, back_short = join((grad_q, back_short), sb1, sc1)
    sq1 = Line(scatter_chunk(*grad_q, 1))
    grad_c = grads_of((back_short, hidden_0))
    pushed_0 = hidden_back(back_short, w_c0, slope_0)
    grad_c, pushed_0 = join((grad_c, pushed_0), sq1)
    sc0 = Line(scatter_chunk(*grad_c, 0))
    grad_mid_0, proj_0, sums_mid, columns_mid = norm_back(
        5, grad_layer, pushed_0, w_b0, middle_0, tables[0]
    )
    above_0 = attended_back(proj_0, w_a0)
    grad_bo = grads_of((short_0, pushed_0), (proj_0, attended_0))
    result = from_own(hidden_down(middle_1, hidden_1, w_c1, tables[1]))
    grad_bo, result, above_0 = join((grad_bo, result, above_0), sc0, sq1, sc1)
    out = Line(iter_swaps(result, first, side, 1))
    sb0 = Line(scatter_chunk(*grad_bo, 0))
    near_a, far_a = attend_back(query_0, own_0, other_0, biases, logs_0, above_0, 0)
    near_a, far_a, above_0 = join((near_a, far_a, above_0), sb0, sc0, sq1, sb1, out)
    near_b, far_b = attend_back(query_0, own_0, other_0, biases, logs_0, above_0, 1)
    near_b, far_a, far_b = join((near_b, far_a, far_b), sb0, sc0, sb1, sc1)
    far_a, far_b = swap(far_a, "section"), swap(far_b, "section")
    flat_0 = flat_of((near_a, near_b), (far_a, far_b))
    grad_values, _, sums_in, columns_in = norm_back(
        0, grad_mid_0, flat_0, w_a0, values, tables[0]
    )
    table_0 = table_back(turned, sums_in, columns_in, sums_mid, columns_mid, order_low)
    grad_q = grads_of((normed_0, flat_0), extra=(table_0,))
    grad_q = join(grad_q, sb0, sc0, sq1, out)
    sq0 = Line(scatter_chunk(*grad_q, 0))
    into = Line(iter_swaps(from_own(grad_values), first, side, 0), sq0.sent)
    join((), sq0, sc0, sq1)
    join((), sq0, into)
    join((), sq0, sb0)
    lines = [sq0, into, out, sb0, sc0, sq1, sb1, sc1]
    while any(not line.done for line in lines):
        join((), *lines)

    boundary = jnp.where(first, into.result, out.result)

    def cut_up(total, sizes):
        parts, start = [], 0
        for size in sizes:
            parts.append(total[:, start : start + size])
            start += size
        return parts

    three = 3 * third

    def sorted_parts(c, bo, qv):
        return (*cut_up(qv, (three, 128)), *cut_up(bo, (unit, third)), c)

    sums_0 = (sc0.result, sb0.result, sq0.result)
    sums_1 = (sc1.result, sb1.result, sq1.result)
    mine = [sorted_parts(*(total for total, _ in sums)) for sums in (sums_0, sums_1)]
    came = [sorted_parts(*(part for _, part in sums)) for sums in (sums_0, sums_1)]
    grads = [
        jnp.where(first, jnp.concatenate([g, g_far]), jnp.concatenate([h_far, h]))
        for g, g_far, h, h_far in zip(mine[0], came[0], mine[1], came[1])
    ]
    g_q, g_v, g_b, g_o, g_c = grads
    table_grad = lax.dynamic_slice_in_dim(g_v[:, :12], side * cut, cut, 0).T
    return (
        boundary[None],
        table_grad[None],
        g_q.reshape(w_qkv.shape),
        g_o.T[None],
        g_b[None],
        g_c.T[None],
    )


def solution(mesh):
    in_specs = (
        P("section", "dp", "tensor", None),
        P("dp"),
        P("section", None, ("dp", "tensor")),
        P("section", "dp", None, "tensor"),
        P("section", "tensor", "dp"),
        P("section", "dp", "tensor"),
        P("section", "tensor", "dp"),
    )
    out_specs = (
        P("section", "dp", "tensor", None),
        P("section", None, ("dp", "tensor")),
        P("section", "dp", None, "tensor"),
        P("section", "tensor", "dp"),
        P("section", "dp", "tensor"),
        P("section", "tensor", "dp"),
    )
    return jax.shard_map(body, mesh=mesh, in_specs=in_specs, out_specs=out_specs, check_vma=False)
```

```python
from functools import partial

import jax
import jax.numpy as jnp
from jax import lax
from jax.experimental import pallas as pl
from jax.experimental.pallas import tpu as pltpu
from jax.sharding import PartitionSpec as P

BF16 = jnp.bfloat16
F32 = jnp.float32
ROWS = (((0,), (0,)), ((), ()))
COLS = (((1,), (1,)), ((), ()))
PLAIN = (((1,), (0,)), ((), ()))
CROSS = ((0, 1), (1, 0))


def cost(flops, size, exps=0):
    return pl.CostEstimate(flops=flops, bytes_accessed=size, transcendentals=exps)


def dot(left, right, dims=PLAIN):
    return lax.dot_general(left, right, dims, preferred_element_type=F32)


def swap(array, axis):
    return lax.ppermute(array, axis, CROSS)


def pair_swap(array, bit=1):
    return lax.ppermute(array, "dp", [(i, i ^ bit) for i in range(lax.axis_size("dp"))])


def ring_shift(array, by):
    ring = lax.axis_size("dp") // 2
    pairs = [(2 * z + x, 2 * ((z + by) % ring) + x) for z in range(ring) for x in (0, 1)]
    return lax.ppermute(array, "dp", pairs)


def tied(state, after):
    return lax.optimization_barrier((state, after))[0] if after else state


class Line:
    def __init__(self, steps, after=()):
        self.steps, self.result, self.done = steps, None, False
        self.take(next(steps), after)

    def take(self, step, after):
        self.sent = tied([array for _, array in step], after)
        self.pending = [send(array) for (send, _), array in zip(step, self.sent)]

    def advance(self, arrays, after):
        try:
            self.take(self.steps.send(arrays), after)
        except StopIteration as end:
            self.result, self.done, self.pending, self.sent = end.value, True, [], []


def join(state, *lines):
    lines = [line for line in lines if not line.done]
    state, arrays = lax.optimization_barrier((state, [line.pending for line in lines]))
    sent = []
    for line, own in zip(lines, arrays):
        line.advance(own, sent)
        sent = sent + line.sent
    return tied(state, sent)


def over(axis):
    return lambda array: swap(array, axis)


def around(by):
    return lambda array: ring_shift(array, by)


def ring_gather(piece):
    ring = lax.axis_size("dp") // 2
    if ring <= 4:
        came = yield [(around(k), piece) for k in range(1, ring)]
        return [piece, *came]

    def step(k, state):
        moving, held = state
        moving = ring_shift(moving, 1)
        return moving, lax.dynamic_update_index_in_dim(held, moving, k, 0)

    held = jnp.zeros((ring,) + piece.shape, piece.dtype).at[0].set(piece)
    held = lax.fori_loop(1, ring, step, (piece, held))[1]
    return [held.reshape(-1, piece.shape[1])]


def ring_scatter(parts):
    ring = len(parts)
    if ring <= 4:
        came = yield [(around(-k), parts[k]) for k in range(1, ring)]
        return sum((part.astype(F32) for part in came), parts[0])

    stacked = jnp.stack([part.astype(BF16) for part in parts[1:]])

    def step(k, total):
        mine = lax.dynamic_index_in_dim(stacked, ring - 2 - k, 0, keepdims=False)
        return mine.astype(F32) + ring_shift(total.astype(BF16), -1).astype(F32)

    total = lax.fori_loop(1, ring - 1, step, stacked[ring - 2].astype(F32))
    return parts[0] + ring_shift(total.astype(BF16), -1).astype(F32)


def copy_kernel(plan, count, *refs):
    sources, outs, sems = refs[:count], refs[count:-1], refs[-1]
    copies = []
    for source, (out, row) in zip(sources, plan):
        copies.append(
            pltpu.make_async_copy(
                source, outs[out].at[pl.ds(row, source.shape[0])], sems.at[len(copies)]
            )
        )
    for copy in copies:
        copy.start()
    for copy in copies:
        copy.wait()


def stack_rows(*groups):
    sources = [part for group in groups for part in group]
    plan, outs = [], []
    for index, group in enumerate(groups):
        row = 0
        for part in group:
            plan.append((index, row))
            row += part.shape[0]
        outs.append(jax.ShapeDtypeStruct((row,) + group[0].shape[1:], group[0].dtype))
    return pl.pallas_call(
        partial(copy_kernel, plan, len(sources)),
        out_shape=outs,
        in_specs=[pl.BlockSpec(memory_space=pl.ANY)] * len(sources),
        out_specs=[pl.BlockSpec(memory_space=pltpu.VMEM)] * len(outs),
        scratch_shapes=[pltpu.SemaphoreType.DMA((len(sources),))],
        compiler_params=pltpu.CompilerParams(vmem_limit_bytes=(1 << 20) + sum(2 * out.size for out in outs)),
        cost_estimate=cost(0, sum(4 * part.size for part in sources)),
        name="stack_rows",
    )(*sources)


def gather_chunk(piece):
    rows, columns = piece.shape
    low = (lax.axis_size("dp") // 4) * rows
    near = yield from ring_gather(piece)
    near = stack_rows(near)[0] if len(near) > 1 and rows % 16 == 0 else jnp.concatenate(near)
    over_x, over_y = yield [(pair_swap, near), (over("tensor"), near)]
    first, second = yield [(over("tensor"), over_x[:low]), (pair_swap, over_y[low:])]
    mine = stack_rows([near, over_x, over_y, first, second])[0]
    mine = mine.reshape(2, -1, columns)
    (theirs,) = yield [(over("section"), mine)]
    return stack_rows([mine[0], theirs[0]], [mine[1], theirs[1]])


def pick_kernel(ring, column, place, mine, theirs, out0, out1, sems):
    z, x, y = place[0], place[1], place[2]
    rows, columns = mine.shape[1], out0.shape[1]
    copies = []
    for ds, source in enumerate((mine, theirs)):
        for dx in (0, 1):
            for k in range(ring):
                owner = 2 * lax.rem(z - k + ring, ring) + (x + dx) % 2
                row = ((ds * 2 + dx) * ring + k) * rows
                for dy, out in enumerate((out0, out1)):
                    copies.append(
                        pltpu.make_async_copy(
                            source.at[2 * owner + (y + dy) % 2, :, pl.ds(column, columns)],
                            out.at[pl.ds(row, rows)],
                            sems.at[len(copies)],
                        )
                    )
    for copy in copies:
        copy.start()
    for copy in copies:
        copy.wait()


def pick(place, mine, theirs, column, columns):
    groups, rows, _ = mine.shape
    ring = groups // 4
    if rows % 16:
        return pick_plain(place, mine, theirs, column, columns)
    out = like((groups * rows, columns))
    return pl.pallas_call(
        partial(pick_kernel, ring, column),
        out_shape=[out, out],
        in_specs=[pl.BlockSpec(memory_space=pltpu.SMEM)] + [pl.BlockSpec(memory_space=pl.ANY)] * 2,
        out_specs=[pl.BlockSpec(memory_space=pltpu.VMEM)] * 2,
        scratch_shapes=[pltpu.SemaphoreType.DMA((2 * groups,))],
        compiler_params=pltpu.CompilerParams(vmem_limit_bytes=6 * 1024 * 1024),
        cost_estimate=cost(0, 4 * groups * rows * columns),
        name="pick",
    )(place, mine, theirs)


def pick_plain(place, mine, theirs, column, columns):
    groups, rows, _ = mine.shape
    ring = groups // 4
    near = jnp.arange(groups // 2) % ring
    owner = 2 * ((place[0] - near + ring) % ring) + (place[1] + jnp.arange(groups // 2) // ring) % 2
    outs = []
    for dy in (0, 1):
        which = 2 * owner + (place[2] + dy) % 2
        parts = [part[:, :, column : column + columns][which] for part in (mine, theirs)]
        outs.append(jnp.concatenate(parts).reshape(-1, columns))
    return outs


def total_of(own, came):
    return own[0].astype(F32) + came[0].astype(F32)


def corner_kernel(low, own, came, first, second):
    total = total_of(own, came)
    first[...] = total[:low].astype(BF16)
    second[...] = total[low:].astype(BF16)


def sides_kernel(low, own_x, came_x, own_y, came_y, first, second, over_x, over_y):
    total = total_of(own_x, came_x)
    over_x[:low] = (total[:low] + first[...].astype(F32)).astype(BF16)
    over_x[low:] = total[low:].astype(BF16)
    total = total_of(own_y, came_y)
    over_y[:low] = total[:low].astype(BF16)
    over_y[low:] = (total[low:] + second[...].astype(F32)).astype(BF16)


def near_kernel(own, came, over_x, over_y, *near):
    total = total_of(own, came) + over_x[...].astype(F32) + over_y[...].astype(F32)
    rows = near[0].shape[0]
    for k, out in enumerate(near):
        out[...] = total[k * rows : (k + 1) * rows].astype(out.dtype)


def call(kernel, name, ins, outs, flops=0, exps=0, limit=5, specs=None, aliases=None):
    size = lambda a: a.size * a.dtype.itemsize
    return pl.pallas_call(
        kernel,
        out_shape=outs,
        in_specs=specs or [pl.BlockSpec(memory_space=pltpu.VMEM)] * len(ins),
        out_specs=[pl.BlockSpec(memory_space=pltpu.VMEM)] * len(outs),
        compiler_params=pltpu.CompilerParams(vmem_limit_bytes=limit * 1024 * 1024),
        cost_estimate=cost(flops, sum(size(a) for a in ins) + sum(size(o) for o in outs), exps),
        name=name,
    )(*ins)


def like(shape, kind=BF16):
    return jax.ShapeDtypeStruct(shape, kind)


def scatter_chunk(own, other, core):
    ring = lax.axis_size("dp") // 2
    columns = own.shape[2]
    quarter = own.shape[1] // 2
    rows = quarter // ring
    low = (ring // 2) * rows
    (came,) = yield [(over("section"), other)]
    block = lambda t, x: pl.BlockSpec((1, quarter, columns), lambda i: (t, x, 0))
    whole = lambda size: pl.BlockSpec((size, columns), lambda i: (0, 0))

    def run(kernel, name, blocks, extra, outs):
        ins = [array for _ in blocks for array in (own, came)] + extra
        specs = [block(*spot) for spot in blocks for _ in (0, 1)]
        return pl.pallas_call(
            kernel,
            grid=(1,),
            out_shape=outs,
            in_specs=specs + [whole(array.shape[0]) for array in extra],
            out_specs=[whole(out.shape[0]) for out in outs],
            compiler_params=pltpu.CompilerParams(vmem_limit_bytes=14 * 1024 * 1024),
            cost_estimate=cost(0, 6 * quarter * columns * len(blocks)),
            name=name,
        )(*ins)

    first, second = run(
        partial(corner_kernel, low), "corner", [(1, 1)], [],
        [like((low, columns)), like((quarter - low, columns))],
    )
    first, second = yield [(over("tensor"), first), (pair_swap, second)]
    over_x, over_y = run(
        partial(sides_kernel, low), "sides", [(0, 1), (1, 0)], [first, second],
        [like((quarter, columns))] * 2,
    )
    over_x, over_y = yield [(pair_swap, over_x), (over("tensor"), over_y)]
    kinds = [F32] + [BF16] * (ring - 1)
    near = run(
        near_kernel, "near", [(0, 0)], [over_x, over_y], [like((rows, columns), k) for k in kinds]
    )
    total = yield from ring_scatter(near)
    to_core = lambda array: lax.ppermute(array, "section", [(1 - core, core)])
    (came,) = yield [(to_core, total.astype(BF16))]
    return total, came.astype(F32)


def attend_kernel(scale, q_ref, k0_ref, k1_ref, v0_ref, v1_ref, b0_ref, b1_ref, o_ref, lse_ref):
    span = q_ref.shape[0]
    lane = lax.broadcasted_iota(jnp.int32, (span, 128), 1)
    q = q_ref[...]
    k0, k1 = k0_ref[...], k1_ref[...]
    v0, v1 = v0_ref[...], v1_ref[...]
    b0, b1 = b0_ref[...], b1_ref[...]
    outs = []
    for head in (0, 1):
        own = (lane >= 64 * head) & (lane < 64 * head + 64)
        qh = jnp.where(own, q * jnp.asarray(scale, BF16), jnp.zeros_like(q))
        s0 = dot(k0, qh, COLS) + b0
        s1 = dot(k1, qh, COLS) + b1
        peak = jnp.maximum(jnp.max(s0, 0, keepdims=True), jnp.max(s1, 0, keepdims=True))
        p0 = jnp.exp(s0 - peak)
        p1 = jnp.exp(s1 - peak)
        total = jnp.sum(p0, 0, keepdims=True) + jnp.sum(p1, 0, keepdims=True)
        out = dot(v0, p0.astype(BF16), ROWS) + dot(v1, p1.astype(BF16), ROWS)
        outs.append(out / total)
        lse_ref[0, head : head + 1, :] = peak + jnp.log(total)
    row = lax.broadcasted_iota(jnp.int32, (128, span), 0)
    o_ref[...] = jnp.where(row < 64, outs[0], outs[1]).T.astype(BF16)


def attend(query, own, other, biases):
    _, span, width = query.shape
    groups = width // 128
    block = lambda first: pl.BlockSpec((None, span, 128), lambda t, g: (t, 0, first * groups + g))
    bias = pl.BlockSpec((span, 1), lambda t, g: (0, 0))
    return pl.pallas_call(
        partial(attend_kernel, 0.125),
        grid=(2, groups),
        out_shape=[like(query.shape), like((2, groups, 8, span), F32)],
        in_specs=[block(0), block(0), block(0), block(1), block(1), bias, bias],
        out_specs=[block(0), pl.BlockSpec((None, 1, 8, span), lambda t, g: (t, g, 0, 0))],
        compiler_params=pltpu.CompilerParams(vmem_limit_bytes=9 * 1024 * 1024),
        cost_estimate=cost(32 * groups * span * span * 2 * 128, 16 * span * width, 8 * groups * span * span),
        name="attend",
    )(query, own, other, own, other, *biases)


def attend_back_kernel(
    scale, q_ref, k0_ref, k1_ref, v0_ref, v1_ref, b0_ref, b1_ref, lse_ref, do_ref,
    near_ref, far_ref,
):
    span = q_ref.shape[0]
    lane = lax.broadcasted_iota(jnp.int32, (span, 128), 1)
    q, above = q_ref[...], do_ref[...]
    keys = (k0_ref[...], k1_ref[...])
    values = (v0_ref[...], v1_ref[...])
    biases = (b0_ref[...], b1_ref[...])
    dqs, dks, dvs = [], [], []
    for head in (0, 1):
        own = (lane >= 64 * head) & (lane < 64 * head + 64)
        qh = jnp.where(own, q * jnp.asarray(scale, BF16), jnp.zeros_like(q))
        ah = jnp.where(own, above, jnp.zeros_like(above))
        lse = lse_ref[0, head : head + 1, :]
        probs, pushed = [], []
        for part in (0, 1):
            probs.append(jnp.exp(dot(keys[part], qh, COLS) + biases[part] - lse))
            pushed.append(dot(values[part], ah, COLS))
        inner = jnp.sum(probs[0] * pushed[0], 0, keepdims=True) + jnp.sum(
            probs[1] * pushed[1], 0, keepdims=True
        )
        dq = None
        for part in (0, 1):
            slopes = (probs[part] * (pushed[part] - inner)).astype(BF16)
            piece = dot(keys[part], slopes, ROWS)
            dq = piece if dq is None else dq + piece
            dk = dot(slopes, qh)
            dv = dot(probs[part].astype(BF16), ah)
            if head == 0:
                dks.append(dk)
                dvs.append(dv)
            else:
                dks[part] = dks[part] + dk
                dvs[part] = dvs[part] + dv
        dqs.append(dq)
    row = lax.broadcasted_iota(jnp.int32, (128, span), 0)
    near_ref[0] = (jnp.where(row < 64, dqs[0], dqs[1]) * scale).T.astype(BF16)
    near_ref[1] = dks[0].astype(BF16)
    near_ref[2] = dvs[0].astype(BF16)
    far_ref[0] = dks[1].astype(BF16)
    far_ref[1] = dvs[1].astype(BF16)


def attend_back(query, own, other, biases, lse, above, t):
    _, span, width = query.shape
    groups = width // 128
    block = lambda first: pl.BlockSpec((None, span, 128), lambda g: (t, 0, first * groups + g))
    bias = pl.BlockSpec((span, 1), lambda g: (0, 0))
    return pl.pallas_call(
        partial(attend_back_kernel, 0.125),
        grid=(groups,),
        out_shape=[like((3, span, width)), like((2, span, width))],
        in_specs=[block(0), block(0), block(0), block(1), block(1), bias, bias]
        + [pl.BlockSpec((None, 1, 8, span), lambda g: (t, g, 0, 0)), block(0)],
        out_specs=[
            pl.BlockSpec((3, span, 128), lambda g: (0, 0, g)),
            pl.BlockSpec((2, span, 128), lambda g: (0, 0, g)),
        ],
        compiler_params=pltpu.CompilerParams(vmem_limit_bytes=14 * 1024 * 1024),
        cost_estimate=cost(40 * groups * span * span * 2 * 128, 12 * span * width, 4 * groups * span * span),
        name="attend_back",
    )(query, own, other, own, other, *biases, lse, above)


def normalised(values):
    centred = values - jnp.mean(values, -1, keepdims=True)
    scale = lax.rsqrt(jnp.mean(centred * centred, -1, keepdims=True) + 1e-05)
    return centred * scale, scale


def mixed_kernel(values, w0, w1, table, normed, query, own):
    third = query.shape[2]
    unit, _ = normalised(values[...])
    rows = (unit * (1.0 + table[0:1]) + table[1:2]).astype(BF16)
    normed[...] = rows
    for t, weight in enumerate((w0, w1)):
        cut = pl.ds(t * third, third)
        query[t] = (dot(rows, weight[:, :third]) + table[2:3, cut]).astype(BF16)
        own[t, :, :third] = dot(rows, weight[:, third : 2 * third]).astype(BF16)
        own[t, :, third:] = (dot(rows, weight[:, 2 * third : 3 * third]) + table[3:4, cut]).astype(BF16)


def mixed_forward(values, w_a, table):
    span, width = values.shape
    third = w_a[0].shape[1] // 4
    outs = [like((span, width)), like((2, span, third)), like((2, span, 2 * third))]
    return call(mixed_kernel, "mixed", [values, *w_a, table], outs, 2 * span * width * 6 * third)


def middle_kernel(values, attended, w0, w1, table, middle, normed):
    third = attended.shape[2]
    total = values[...] + table[4:5]
    for t, weight in enumerate((w0, w1)):
        total = total + dot(attended[t], weight[:, 3 * third :], COLS)
    middle[...] = total
    unit, _ = normalised(total)
    normed[...] = (unit * (1.0 + table[5:6]) + table[6:7]).astype(BF16)


def middle_forward(values, attended, w_a, table):
    span, width = values.shape
    outs = [like((span, width), F32), like((span, width))]
    return call(
        middle_kernel, "middle", [values, attended, *w_a, table], outs, 2 * span * width * width
    )


def hidden_kernel(normed, w0, w1, table, hidden, slope):
    width = table.shape[1]
    rows = normed[...]
    step = width // 2
    for t, weight in enumerate((w0, w1)):
        for start in range(0, hidden.shape[2], step):
            cut = slice(start, start + step)
            row = 8 + (t * hidden.shape[2] + start) // width
            column = (t * hidden.shape[2] + start) % width
            before = dot(rows, weight[:, cut]) + table[row : row + 1, column : column + step]
            share = 0.5 + 0.5 * lax.erf(before * (0.5**0.5))
            hidden[t, :, cut] = (before * share).astype(BF16)
            bell = jnp.exp(-0.5 * before * before) * 0.3989422804014327
            slope[t, :, cut] = (share + before * bell).astype(BF16)


def hidden_forward(normed, w_b, table):
    span, width = normed.shape
    unit = w_b[0].shape[1]
    outs = [like((2, span, unit))] * 2
    flops, exps = 4 * span * width * unit, 4 * span * unit
    return call(hidden_kernel, "hidden", [normed, *w_b, table], outs, flops, exps)


def down_kernel(middle, hidden, w0, w1, table, out):
    total = middle[...] + table[7:8]
    for t, weight in enumerate((w0, w1)):
        total = total + dot(hidden[t], weight[...], COLS)
    out[...] = total


def hidden_down(middle, hidden, w_c, table):
    span, width = middle.shape
    flops = 4 * span * width * w_c[0].shape[1]
    return call(down_kernel, "down", [middle, hidden, *w_c, table], [like((span, width), F32)], flops)[0]


def slope_kernel(short, w0, w1, slope, pushed):
    rows = short[...]
    step = rows.shape[1] // 2
    for t, weight in enumerate((w0, w1)):
        for start in range(0, slope.shape[2], step):
            cut = slice(start, start + step)
            grad = dot(rows, weight[:, cut]) * slope[t, :, cut].astype(F32)
            pushed[t, :, cut] = grad.astype(BF16)


def hidden_back(short, w_c, slope):
    flops = 2 * short.shape[1] * slope.size
    return call(slope_kernel, "hidden_back", [short, *w_c, slope], [like(slope.shape)], flops)[0]


def grads_kernel(count, *refs):
    outs = refs[-2:]
    start = 0
    for left, right in zip(refs[:count], refs[count : 2 * count]):
        half, size = left.shape[1] // 2, right.shape[2]
        for core, out in enumerate(outs):
            rows = left[:, core * half : (core + 1) * half].T
            for t in (0, 1):
                out[t, :, start : start + size] = dot(rows, right[t]).astype(BF16)
        start += size
    if len(refs) > 2 * count + 2:
        extra = refs[2 * count]
        half, size = extra.shape[0] // 2, extra.shape[1]
        for core, out in enumerate(outs):
            for t in (0, 1):
                out[t, :, start:] = extra[core * half : (core + 1) * half]


def grads_of(*pairs, extra=()):
    lefts, rights = [pair[0] for pair in pairs], [pair[1] for pair in pairs]
    half = lefts[0].shape[1] // 2
    total = sum(right.shape[2] for right in rights)
    flops = 8 * half * lefts[0].shape[0] * total
    total += sum(part.shape[1] for part in extra)
    outs = [like((2, half, total))] * 2
    ins = lefts + rights + list(extra)
    return call(partial(grads_kernel, len(pairs)), "grads", ins, outs, flops, limit=6)


def flat_kernel(near0, far0, near1, far1, flat):
    third = near0.shape[2]
    for t, (near, far) in enumerate(((near0, far0), (near1, far1))):
        for n in range(3):
            part = near[n]
            if n:
                part = (part.astype(F32) + far[n - 1].astype(F32)).astype(BF16)
            flat[t, :, n * third : (n + 1) * third] = part


def flat_of(near, far):
    _, span, third = near[0].shape
    ins = [near[0], far[0], near[1], far[1]]
    return call(flat_kernel, "flat", ins, [like((2, span, 3 * third))])[0]


def norm_back_kernel(gain, tail, add, parts, w0, w1, values, table, out, short, sums, columns, *above):
    size = parts.shape[2]
    weights = (w0, w1)
    grad = sum(dot(parts[t], weights[t][:, :size], COLS) for t in (0, 1))
    unit, scale = normalised(values[...])
    inner = grad * (1.0 + table[gain : gain + 1])
    inner = inner - jnp.mean(inner, -1, keepdims=True)
    inner = inner - unit * jnp.mean(inner * unit, -1, keepdims=True)
    total = add[...] + inner * scale
    out[...] = total
    low = total.astype(BF16)
    short[...] = low
    sums[0:1] = jnp.sum(grad * unit, 0, keepdims=True)
    sums[1:2] = jnp.sum(grad, 0, keepdims=True)
    sums[2:3] = jnp.sum(total, 0, keepdims=True)
    sums[3:4] = jnp.sum(add[...], 0, keepdims=True)
    for t in (0, 1):
        columns[t, 0:1] = jnp.sum(parts[t].astype(F32), 0, keepdims=True)


def norm_back(gain, add, parts, weights, values, table):
    span, width = values.shape
    size = parts.shape[2]
    outs = [
        like((span, width), F32), like((span, width)), like((8, width), F32), like((2, 8, size), F32),
    ]
    ins = [add, parts, *weights, values, table]
    return call(
        partial(norm_back_kernel, gain, 0), "norm_back", ins, outs, 4 * span * width * size
    )


def above_kernel(short, w0, w1, above):
    third = above.shape[2]
    for t, weight in enumerate((w0, w1)):
        above[t] = dot(short[...], weight[:, 3 * third :]).astype(BF16)


def attended_back(short, w_a):
    span, width = short.shape
    third = w_a[0].shape[1] // 4
    flops = 4 * span * width * third
    return call(above_kernel, "above", [short, *w_a], [like((2, span, third))], flops)[0]


def table_kernel(side, sums_in, columns_in, sums_mid, columns_mid, order, out):
    third = columns_in.shape[2] // 3
    width = order.shape[0]
    swapped = side[0] != 0

    def halves(parts):
        first = jnp.where(swapped, parts[1], parts[0])
        second = jnp.where(swapped, parts[0], parts[1])
        return [first, second]

    query = jnp.concatenate(halves([columns_in[t, 0:1, :third] for t in (0, 1)]), 1)
    value = jnp.concatenate(halves([columns_in[t, 0:1, 2 * third :] for t in (0, 1)]), 1)
    rise = halves([columns_mid[t, 0:1, :] for t in (0, 1)])
    rows = [query, value]
    for part in rise:
        rows += [part[:, :width], part[:, width:]]
    rows = jnp.concatenate(rows + [jnp.zeros((2, width), F32)], 0)
    rows = dot(rows.astype(BF16), order[...])
    table = [
        sums_in[0:2], rows[0:2], sums_mid[2:3], sums_mid[0:2], sums_mid[3:4], rows[2:6],
        jnp.zeros((out.shape[1] - 12, width), F32),
    ]
    out[...] = jnp.concatenate(table, 0).T.astype(BF16)


def table_back(side, sums_in, columns_in, sums_mid, columns_mid, order):
    ins = [side, sums_in, columns_in, sums_mid, columns_mid, order]
    specs = [pl.BlockSpec(memory_space=pltpu.SMEM)] + [pl.BlockSpec(memory_space=pltpu.VMEM)] * 5
    outs = [like((order.shape[0], 128))]
    return call(table_kernel, "table_back", ins, outs, specs=specs)[0]


def iter_swaps(rows, first, side, core):
    span, width = rows.shape
    to_core = lambda array: lax.ppermute(array, "section", [(1 - core, core)])
    (came,) = yield [(to_core, rows.astype(BF16))]
    came = came.astype(F32)
    full = jnp.stack([rows, came] if core == 0 else [came, rows])
    keep = lax.dynamic_index_in_dim(full, side, 0, keepdims=False)
    gone = lax.dynamic_index_in_dim(full, 1 - side, 0, keepdims=False).astype(BF16)
    pairs = [(2 * core, 2 * core + 1), (2 * core + 1, 2 * core)]
    (came,) = yield [(lambda array: lax.ppermute(array, ("section", "tensor"), pairs), gone)]
    came = came.astype(F32)
    return jnp.where(side == 0, jnp.stack([keep, came]), jnp.stack([came, keep]))


FEATURE_ROWS = (True, True, False, False, True, True, True, True, False, False, False, False)


def body(ends_in, lengths, vectors, w_qkv, w_out, w_up, w_down):
    core = lax.axis_index("section")
    first = core == 0
    side = lax.axis_index("tensor")
    count = lax.axis_size("dp")
    ring = count // 2
    rows = w_qkv.shape[1]
    half = rows // 2
    span, width = ends_in.shape[2:]
    third, unit = w_qkv.shape[-1], w_up.shape[-1]
    turned = side.astype(jnp.int32).reshape(1)

    at = jnp.arange(width, dtype=jnp.int32)
    row, rest = at % half, at // half
    step, rest = rest % ring, rest // ring
    spot = lax.axis_index("dp")
    owner = 2 * ((spot // 2 - step + ring) % ring) + (spot % 2 + rest % 2) % 2
    source = owner * rows + ((core + rest // 2) % 2) * half + row
    order = at[:, None] == source[None, :]
    order_low = order.astype(BF16)

    def to_own(array):
        return jnp.dot(array, order.astype(F32), precision=lax.Precision.HIGHEST)

    def from_own(array):
        return lax.dot_general(array, order.astype(F32), COLS, precision=lax.Precision.HIGHEST)

    index = spot * 2 + side
    cut = vectors.shape[-1]
    spread = lax.dynamic_update_slice_in_dim(
        jnp.zeros((vectors.shape[1], width), F32), vectors[0], index * cut, 1
    )
    own = jnp.concatenate([w_qkv[0].reshape(rows, -1), w_out[0].T, w_up[0], w_down[0].T], 1)
    halves = (own[:half], own[half:])
    came = swap(jnp.where(first, halves[1], halves[0]), "section")
    one, two = jnp.where(first, halves[0], came), jnp.where(first, came, halves[1])
    cuts = [slice(n * unit, (n + 1) * unit) for n in range(3)]
    chunks = [layer[:, c] for layer in (one,) for c in cuts]
    far_mine = lax.all_gather(two[:, : 2 * unit], ("dp", "tensor"), axis=0)
    a0 = Line(gather_chunk(chunks[0]))
    spread, ends = tied((spread, ends_in[0]), a0.sent)
    spread = spread + swap(spread, "tensor")
    spread, ends = lax.optimization_barrier((spread, ends))

    keep = lax.dynamic_index_in_dim(ends, side, 0, keepdims=False)
    gone = lax.dynamic_index_in_dim(ends, 1 - side, 0, keepdims=False)
    clip = swap(gone, "tensor")
    bit = 1
    while bit < count:
        spread = spread + pair_swap(spread, bit)
        bit *= 2
    theirs = swap(spread, "section")
    spread, theirs, clip, ready = join((spread, theirs, clip, chunks[1]), a0)
    b0 = Line(gather_chunk(ready))
    upper, lower = jnp.where(side == 0, keep, clip), jnp.where(side == 0, clip, keep)
    stay, leave = jnp.where(first, upper, lower), jnp.where(first, lower, upper)
    came = swap(leave, "section")
    values = dot(jnp.where(first, stay, came), order_low)
    upstream = dot(jnp.where(first, came, stay), order_low)
    up_short = upstream.astype(BF16)
    frames = lax.dynamic_index_in_dim(lengths, side, 0, keepdims=False)
    spots = lax.broadcasted_iota(jnp.int32, (span, 1), 0)
    biases = [
        jnp.where(spots + offset * span < frames, 0.0, -1e30).astype(F32)
        for offset in (core, 1 - core)
    ]
    is_feature = jnp.array(FEATURE_ROWS)[:, None]

    def sides_turned(table):
        heads = table[:8].reshape(8, 2, -1)
        rise = table[8:].reshape(2, 2, width)
        heads = jnp.where(side == 0, heads, heads[:, ::-1]).reshape(8, width)
        rise = jnp.where(side == 0, rise, rise[::-1]).reshape(4, width)
        return jnp.concatenate([heads, rise])

    def own_table(table):
        return jnp.where(is_feature, to_own(table), sides_turned(table))

    tables = [
        own_table(jnp.where(first, spread, theirs)),
        own_table(jnp.where(first, theirs, spread)),
    ]

    values, upstream, up_short, tables, ready = join(
        (values, upstream, up_short, tables, chunks[2]), a0, b0
    )
    c0 = Line(gather_chunk(ready))
    join((), a0)
    join((), a0, b0)
    w_a0 = a0.result
    normed_0, query_0, own_0 = mixed_forward(values, w_a0, tables[0])
    other_0 = swap(own_0, "section")
    query_0, own_0, other_0 = tied((query_0, own_0, other_0), b0.sent)
    attended_0, logs_0 = attend(query_0, own_0, other_0, biases)
    attended_0 = join(attended_0, b0, c0)
    middle_0, short_0 = middle_forward(values, attended_0, w_a0, tables[0])
    short_0 = join(short_0, b0)
    w_b0 = b0.result
    hidden_0, slope_0 = hidden_forward(short_0, w_b0, tables[0])
    hidden_0, slope_0, far_mine, ready = join((hidden_0, slope_0, far_mine, two[:, 2 * unit :]), c0)
    far_theirs = swap(far_mine, "section")
    c1 = Line(gather_chunk(ready))
    join((), c0)
    hidden_0 = join(hidden_0, c0)
    w_c0 = c0.result
    layer_one = hidden_down(middle_0, hidden_0, w_c0, tables[0])
    place = jnp.stack([spot // 2, spot % 2, side]).astype(jnp.int32)
    layer_one = join(layer_one, c1)
    w_a1, w_b1 = (pick(place, far_mine, far_theirs, n * unit, unit) for n in (0, 1))
    normed_1, query_1, own_1 = mixed_forward(layer_one, w_a1, tables[1])
    other_1 = swap(own_1, "section")
    attended_1, logs_1 = attend(query_1, own_1, other_1, biases)
    attended_1 = join(attended_1, c1)
    middle_1, short_1 = middle_forward(layer_one, attended_1, w_a1, tables[1])
    hidden_1, slope_1 = hidden_forward(short_1, w_b1, tables[1])
    hidden_1, slope_1 = join((hidden_1, slope_1), c1)
    grad_c = grads_of((up_short, hidden_1))
    grad_c = join(grad_c, c1)
    w_c1 = c1.result
    sc1 = Line(scatter_chunk(*grad_c, 1))

    pushed_1 = hidden_back(up_short, w_c1, slope_1)
    pushed_1 = join(pushed_1, sc1)
    grad_mid_1, proj_1, sums_mid, columns_mid = norm_back(
        5, upstream, pushed_1, w_b1, middle_1, tables[1]
    )
    above_1 = attended_back(proj_1, w_a1)
    grad_bo = grads_of((short_1, pushed_1), (proj_1, attended_1))
    grad_bo, above_1 = join((grad_bo, above_1), sc1)
    sb1 = Line(scatter_chunk(*grad_bo, 1))
    near_a, far_a = attend_back(query_1, own_1, other_1, biases, logs_1, above_1, 0)
    near_a, far_a, above_1 = join((near_a, far_a, above_1), sb1, sc1)
    near_b, far_b = attend_back(query_1, own_1, other_1, biases, logs_1, above_1, 1)
    near_b, far_a, far_b = join((near_b, far_a, far_b), sb1)
    far_a, far_b = swap(far_a, "section"), swap(far_b, "section")
    flat_1 = flat_of((near_a, near_b), (far_a, far_b))
    grad_layer, back_short, sums_in, columns_in = norm_back(
        0, grad_mid_1, flat_1, w_a1, layer_one, tables[1]
    )
    table_1 = table_back(turned, sums_in, columns_in, sums_mid, columns_mid, order_low)
    grad_q = grads_of((normed_1, flat_1), extra=(table_1,))
    grad_q, back_short = join((grad_q, back_short), sb1, sc1)
    sq1 = Line(scatter_chunk(*grad_q, 1))
    grad_c = grads_of((back_short, hidden_0))
    pushed_0 = hidden_back(back_short, w_c0, slope_0)
    grad_c, pushed_0 = join((grad_c, pushed_0), sq1, sb1)
    sc0 = Line(scatter_chunk(*grad_c, 0))
    grad_mid_0, proj_0, sums_mid, columns_mid = norm_back(
        5, grad_layer, pushed_0, w_b0, middle_0, tables[0]
    )
    above_0 = attended_back(proj_0, w_a0)
    grad_bo = grads_of((short_0, pushed_0), (proj_0, attended_0))
    result = from_own(hidden_down(middle_1, hidden_1, w_c1, tables[1]))
    grad_bo, result, above_0 = join((grad_bo, result, above_0), sc0, sq1, sc1)
    out = Line(iter_swaps(result, first, side, 1))
    sb0 = Line(scatter_chunk(*grad_bo, 0))
    near_a, far_a = attend_back(query_0, own_0, other_0, biases, logs_0, above_0, 0)
    near_a, far_a, above_0 = join((near_a, far_a, above_0), sb0, sc0, sq1, sb1, out)
    near_b, far_b = attend_back(query_0, own_0, other_0, biases, logs_0, above_0, 1)
    near_b, far_a, far_b = join((near_b, far_a, far_b), sb0, sc0, sb1, sc1)
    far_a, far_b = swap(far_a, "section"), swap(far_b, "section")
    flat_0 = flat_of((near_a, near_b), (far_a, far_b))
    grad_values, _, sums_in, columns_in = norm_back(
        0, grad_mid_0, flat_0, w_a0, values, tables[0]
    )
    table_0 = table_back(turned, sums_in, columns_in, sums_mid, columns_mid, order_low)
    grad_q = grads_of((normed_0, flat_0), extra=(table_0,))
    grad_q = join(grad_q, sb0, sc0, sq1, out)
    sq0 = Line(scatter_chunk(*grad_q, 0))
    into = Line(iter_swaps(from_own(grad_values), first, side, 0), sq0.sent)
    join((), sq0, sc0, sq1)
    join((), sq0, into)
    join((), sq0, sb0)
    lines = [sq0, into, out, sb0, sc0, sq1, sb1, sc1]
    while any(not line.done for line in lines):
        join((), *lines)

    boundary = jnp.where(first, into.result, out.result)

    def cut_up(total, sizes):
        parts, start = [], 0
        for size in sizes:
            parts.append(total[:, start : start + size])
            start += size
        return parts

    three = 3 * third

    def sorted_parts(c, bo, qv):
        return (*cut_up(qv, (three, 128)), *cut_up(bo, (unit, third)), c)

    sums_0 = (sc0.result, sb0.result, sq0.result)
    sums_1 = (sc1.result, sb1.result, sq1.result)
    mine = [sorted_parts(*(total for total, _ in sums)) for sums in (sums_0, sums_1)]
    came = [sorted_parts(*(part for _, part in sums)) for sums in (sums_0, sums_1)]
    grads = [
        jnp.where(first, jnp.concatenate([g, g_far]), jnp.concatenate([h_far, h]))
        for g, g_far, h, h_far in zip(mine[0], came[0], mine[1], came[1])
    ]
    g_q, g_v, g_b, g_o, g_c = grads
    table_grad = lax.dynamic_slice_in_dim(g_v[:, :12], side * cut, cut, 0).T
    return (
        boundary[None],
        table_grad[None],
        g_q.reshape(w_qkv.shape),
        g_o.T[None],
        g_b[None],
        g_c.T[None],
    )


def solution(mesh):
    in_specs = (
        P("section", "dp", "tensor", None),
        P("dp"),
        P("section", None, ("dp", "tensor")),
        P("section", "dp", None, "tensor"),
        P("section", "tensor", "dp"),
        P("section", "dp", "tensor"),
        P("section", "tensor", "dp"),
    )
    out_specs = (
        P("section", "dp", "tensor", None),
        P("section", None, ("dp", "tensor")),
        P("section", "dp", None, "tensor"),
        P("section", "tensor", "dp"),
        P("section", "dp", "tensor"),
        P("section", "tensor", "dp"),
    )
    return jax.shard_map(body, mesh=mesh, in_specs=in_specs, out_specs=out_specs, check_vma=False)
```
